32 devices in a mesh: gx: 2 (over y), gy: 2 (over x), vert: 8 (over z, core).
Axes of the slice: x: 2, y: 2, z: 4, core: 2. Of those that a mesh axis runs over, the one named last changes fastest.
Arguments:
- state: float32 [8000, 3, 4, 256], P('vert', None, 'gy', 'gx'), as said below
- tangent: float32 [8000, 3, 4, 256], P('vert', None, 'gy', 'gx')
- orient: int32 [8000, 2], P('vert'), may hold values from 0 to 1, as said below
- walls: int32 [2, 256], P(None, 'gx'), may hold values from 0 to 1
Outputs:
- product: float32 [8000, 3, 4, 256], P('vert', None, 'gy', 'gx')
The draws below stay inside these ranges and needn't reach their ends.
Inputs may be any that keep to these rules, and one draw needn't show every extreme that they name: In every aligned group of four slots 4k to 4k+3 there are two bits p, r with orient[4k + 2b + e] = (e XOR p, b XOR r) for b, e in 0, 1. The state's values at the four points q of every cell are positive.
All inputs are finite; a program needn't handle non-finite values.
Results may differ from the reference program's by a relative error of at most 0.0003.
Values sent between devices are 32-bit elements; how exact they have to be, the bound alone decides.
No kernel may reach another device: no remote copies, remote signals or barrier semaphores. Data moves between devices by JAX's collectives and lax.ppermute only.
A program may use at most 64 MiB of HBM per device.

```python
import math
import jax
import jax.numpy as jnp
from jax import lax

NVX = 20
NV = 8000
STREAMWISE_SLABS = 256
CROSSWISE_SLABS = 4


def draw_state(key, part):
    half_grid = NVX // 2
    spacing = 5.0 / half_grid
    noise_seedlets = jax.random.split(key, 6)
    slot_index = jnp.arange(NV, dtype=jnp.int32)
    mag_x = (slot_index // (4 * half_grid) % half_grid).astype(jnp.float32) + 0.5
    mag_y = (slot_index // 4 % half_grid).astype(jnp.float32) + 0.5
    level_z = (slot_index // (4 * half_grid * half_grid)).astype(jnp.float32) - (half_grid - 0.5)
    stream_magnitude = ((mag_x * spacing) ** 2 + (mag_y * spacing) ** 2).reshape(NV, 1, 1)
    molecular_grid_extent = (level_z * spacing).reshape(NV, 1, 1)
    thermal_bottom_plate, thermal_roof_plate, jitter_floor, jitter_ceiling, gradient_clamp = (0.7, 1.4, 0.5, 1.5, 0.4)
    thermal_state = jnp.exp(jax.random.uniform(noise_seedlets[0], (1, CROSSWISE_SLABS, STREAMWISE_SLABS), jnp.float32, math.log(thermal_bottom_plate), math.log(thermal_roof_plate)))
    average_offset = jax.random.uniform(noise_seedlets[1], (1, CROSSWISE_SLABS, STREAMWISE_SLABS), jnp.float32, -0.5, 0.5)
    reference_height = jnp.exp(jax.random.uniform(noise_seedlets[2], (1, CROSSWISE_SLABS, STREAMWISE_SLABS), jnp.float32, math.log(0.5), math.log(2.0)))
    streamwise_shape = reference_height * jnp.exp(-(stream_magnitude + (molecular_grid_extent - average_offset) ** 2) / (2.0 * thermal_state)) / (2.0 * math.pi * thermal_state) ** 1.5
    mean_part = streamwise_shape * jax.random.uniform(noise_seedlets[3], (NV, CROSSWISE_SLABS, STREAMWISE_SLABS), jnp.float32, jitter_floor, jitter_ceiling)
    slope_x = mean_part * jax.random.uniform(noise_seedlets[4], (NV, CROSSWISE_SLABS, STREAMWISE_SLABS), jnp.float32, -gradient_clamp, gradient_clamp)
    slope_y = mean_part * jax.random.uniform(noise_seedlets[5], (NV, CROSSWISE_SLABS, STREAMWISE_SLABS), jnp.float32, -gradient_clamp, gradient_clamp)
    return jnp.stack([mean_part, slope_x, slope_y], axis=1)


def draw_tangent(key, part):
    noise_seedlets = jax.random.split(key, 3)
    vel_scale = jnp.exp(jax.random.uniform(noise_seedlets[0], (NV, 1, 1, 1), jnp.float32, math.log(0.1), math.log(1.0)))
    cell_scale = jnp.exp(jax.random.uniform(noise_seedlets[1], (1, 1, CROSSWISE_SLABS, STREAMWISE_SLABS), jnp.float32, math.log(0.3), math.log(3.0)))
    base_draw = jax.random.truncated_normal(noise_seedlets[2], -4.0, 4.0, (NV, 3, CROSSWISE_SLABS, STREAMWISE_SLABS), jnp.float32)
    return base_draw * vel_scale * cell_scale


def draw_orient(key, part):
    flip_bits = jax.random.randint(key, (NV // 4, 2), 0, 2, dtype=jnp.int32)
    slot_index = jnp.arange(NV, dtype=jnp.int32)
    group_index = slot_index // 4
    sign_x = (slot_index % 2 + flip_bits[group_index, 0]) % 2
    sign_y = (slot_index // 2 % 2 + flip_bits[group_index, 1]) % 2
    return jnp.stack([sign_x, sign_y], axis=1).astype(jnp.int32)


def with_ends(values, stream_key, smallest, largest):
    extent = values.shape
    index_at = [jax.random.randint(jax.random.fold_in(stream_key, axis), (), 0, extent[axis]) for axis in range(len(extent))]
    values = values.at[tuple(index_at)].set(smallest)
    longest = extent.index(max(extent))
    index_at[longest] = (index_at[longest] + 1) % extent[longest]
    return values.at[tuple(index_at)].set(largest)


def setup_inputs(seed: int = 0) -> dict:
    key_of = jax.random.split(jax.random.key(seed), 5)
    state = draw_state(jax.random.fold_in(key_of[4], 71), 0)
    tangent = draw_tangent(jax.random.fold_in(key_of[4], 71), 0)
    orient = draw_orient(jax.random.fold_in(key_of[4], 71), 0)
    walls = with_ends(jax.random.randint(key_of[3], (2, STREAMWISE_SLABS), 0, 2), jax.random.fold_in(key_of[3], 1), 0, 1).astype(jnp.int32)
    return dict(state=state, tangent=tangent, orient=orient, walls=walls)


GAUSS = 0.5773502691896258
XI_SIGNS = (-1.0, -1.0, 1.0, 1.0)
ETA_SIGNS = (-1.0, 1.0, -1.0, 1.0)
MIRRORED_DUOS = ((0, 0), (1, 1), (2, 2), (0, 1), (0, 2), (1, 2))
COLLIDE = 2.0
LOG_TWO_PI = math.log(2.0 * math.pi)


def velocities(slot_index, orient, half_grid):
    spacing = 5.0 / half_grid
    mag_x = ((slot_index // (4 * half_grid)) % half_grid).astype(jnp.float32) + 0.5
    mag_y = ((slot_index // 4) % half_grid).astype(jnp.float32) + 0.5
    level_z = (slot_index // (4 * half_grid * half_grid)).astype(jnp.float32) - (half_grid - 0.5)
    sign_x = (2 * orient[:, 0] - 1).astype(jnp.float32)
    sign_y = (2 * orient[:, 1] - 1).astype(jnp.float32)
    return sign_x * mag_x * spacing, sign_y * mag_y * spacing, level_z * spacing


def moment_table(vel_x, vel_y, molecular_grid_extent, weight):
    return jnp.stack([jnp.ones_like(vel_x), vel_x, vel_y, molecular_grid_extent, vel_x * vel_x, vel_y * vel_y,
                      molecular_grid_extent * molecular_grid_extent, vel_x * vel_y, vel_x * molecular_grid_extent, vel_y * molecular_grid_extent]) * weight


def gauss_points(coef):
    center, grad_x, grad_y = coef[:, 0], coef[:, 1], coef[:, 2]
    return jnp.stack([center + XI_SIGNS[q] * GAUSS * grad_x + ETA_SIGNS[q] * GAUSS * grad_y for q in range(4)], axis=1)


def project_points(values):
    total = values[:, 0] + values[:, 1] + values[:, 2] + values[:, 3]
    along_x = (values[:, 2] + values[:, 3]) - (values[:, 0] + values[:, 1])
    along_y = (values[:, 1] + values[:, 3]) - (values[:, 0] + values[:, 2])
    return jnp.stack([0.25 * total, 0.75 * GAUSS * along_x, 0.75 * GAUSS * along_y], axis=1)


def partner(values):
    dims_in = values.shape
    grouped = values.reshape((dims_in[0] // 4, 2, 2) + dims_in[1:])
    return grouped[:, ::-1].reshape(dims_in)


def full_matrix(entries):
    rows = [[None, None, None], [None, None, None], [None, None, None]]
    for duo_ordinal, (leading_multiplier, trailing_multiplier) in enumerate(MIRRORED_DUOS):
        rows[leading_multiplier][trailing_multiplier] = entries[duo_ordinal]
        rows[trailing_multiplier][leading_multiplier] = entries[duo_ordinal]
    return rows


def gauss_params(moments):
    density = moments[0]
    average_offset = [moments[1 + leading_multiplier] / density for leading_multiplier in range(3)]
    second = [moments[4 + duo_ordinal] for duo_ordinal in range(6)]
    covariance_array = [second[duo_ordinal] / density - average_offset[leading_multiplier] * average_offset[trailing_multiplier] for duo_ordinal, (leading_multiplier, trailing_multiplier) in enumerate(MIRRORED_DUOS)]
    thermal_state = (covariance_array[0] + covariance_array[1] + covariance_array[2]) / 3.0
    pressure_dyad = [(1.5 * thermal_state if leading_multiplier == trailing_multiplier else 0.0) - 0.5 * covariance_array[duo_ordinal] for duo_ordinal, (leading_multiplier, trailing_multiplier) in enumerate(MIRRORED_DUOS)]
    tens_full = full_matrix(pressure_dyad)
    cofactor = [tens_full[1][1] * tens_full[2][2] - tens_full[1][2] * tens_full[1][2],
                tens_full[0][0] * tens_full[2][2] - tens_full[0][2] * tens_full[0][2],
                tens_full[0][0] * tens_full[1][1] - tens_full[0][1] * tens_full[0][1],
                tens_full[0][2] * tens_full[1][2] - tens_full[0][1] * tens_full[2][2],
                tens_full[0][1] * tens_full[1][2] - tens_full[0][2] * tens_full[1][1],
                tens_full[0][1] * tens_full[0][2] - tens_full[0][0] * tens_full[1][2]]
    determinant = tens_full[0][0] * cofactor[0] + tens_full[0][1] * cofactor[3] + tens_full[0][2] * cofactor[4]
    inverse = [entry / determinant for entry in cofactor]
    log_pre = jnp.log(density) - 1.5 * LOG_TWO_PI - 0.5 * jnp.log(determinant)
    delta_density = moments[10]
    drift_delta = [(moments[11 + leading_multiplier] - average_offset[leading_multiplier] * delta_density) / density for leading_multiplier in range(3)]
    dtheta = [moments[14 + duo_ordinal] / density - second[duo_ordinal] * delta_density / (density * density)
              - (drift_delta[leading_multiplier] * average_offset[trailing_multiplier] + average_offset[leading_multiplier] * drift_delta[trailing_multiplier]) for duo_ordinal, (leading_multiplier, trailing_multiplier) in enumerate(MIRRORED_DUOS)]
    temp_delta = (dtheta[0] + dtheta[1] + dtheta[2]) / 3.0
    tens_delta = [(1.5 * temp_delta if leading_multiplier == trailing_multiplier else 0.0) - 0.5 * dtheta[duo_ordinal] for duo_ordinal, (leading_multiplier, trailing_multiplier) in enumerate(MIRRORED_DUOS)]
    inv_full = full_matrix(inverse)
    delta_full = full_matrix(tens_delta)
    trace_term = sum([inv_full[leading_multiplier][trailing_multiplier] * delta_full[trailing_multiplier][leading_multiplier] for leading_multiplier in range(3) for trailing_multiplier in range(3)])
    shift_term = delta_density / density - 0.5 * trace_term
    weight_vec = [inv_full[leading_multiplier][0] * drift_delta[0] + inv_full[leading_multiplier][1] * drift_delta[1] + inv_full[leading_multiplier][2] * drift_delta[2] for leading_multiplier in range(3)]
    inner_prod = [[inv_full[leading_multiplier][0] * delta_full[0][c] + inv_full[leading_multiplier][1] * delta_full[1][c] + inv_full[leading_multiplier][2] * delta_full[2][c]
                   for c in range(3)] for leading_multiplier in range(3)]
    curve_sym = [inner_prod[leading_multiplier][0] * inv_full[0][trailing_multiplier] + inner_prod[leading_multiplier][1] * inv_full[1][trailing_multiplier] + inner_prod[leading_multiplier][2] * inv_full[2][trailing_multiplier]
                 for (leading_multiplier, trailing_multiplier) in MIRRORED_DUOS]
    return jnp.stack(average_offset + inverse + [log_pre, shift_term] + weight_vec + curve_sym)


def quadratic(entries, rel_x, rel_y, rel_z):
    return (entries[0] * rel_x * rel_x + entries[1] * rel_y * rel_y + entries[2] * rel_z * rel_z
            + 2.0 * (entries[3] * rel_x * rel_y + entries[4] * rel_x * rel_z + entries[5] * rel_y * rel_z))


def gauss_tangent(vel_x, vel_y, molecular_grid_extent, params):
    rel_x = vel_x[:, None] - params[0]
    rel_y = vel_y[:, None] - params[1]
    rel_z = molecular_grid_extent[:, None] - params[2]
    gauss = jnp.exp(params[9] - 0.5 * quadratic(params[3:9], rel_x, rel_y, rel_z))
    return gauss * (params[10] + rel_x * params[11] + rel_y * params[12] + rel_z * params[13]
                    + 0.5 * quadratic(params[14:20], rel_x, rel_y, rel_z))


def transport(coef, orient, vel_x, vel_y, left_in, right_in, below_in, above_in):
    center, grad_x, grad_y = coef[:, 0], coef[:, 1], coef[:, 2]
    heads_right = (orient[:, 0] == 1)[:, None, None]
    heads_up = (orient[:, 1] == 1)[:, None, None]
    right_val = jnp.where(heads_right, center + grad_x, right_in[0])
    right_slope = jnp.where(heads_right, grad_y, right_in[1])
    left_val = jnp.where(heads_right, left_in[0], center - grad_x)
    left_slope = jnp.where(heads_right, left_in[1], grad_y)
    top_val = jnp.where(heads_up, center + grad_y, above_in[0])
    top_slope = jnp.where(heads_up, grad_x, above_in[1])
    bottom_val = jnp.where(heads_up, below_in[0], center - grad_y)
    bottom_slope = jnp.where(heads_up, below_in[1], grad_x)
    speed_x = vel_x[:, None, None]
    speed_y = vel_y[:, None, None]
    rate_mean = speed_x * (right_val - left_val) + speed_y * (top_val - bottom_val)
    rate_x = 3.0 * speed_x * (right_val + left_val - 2.0 * center) + speed_y * (top_slope - bottom_slope)
    rate_y = speed_x * (right_slope - left_slope) + 3.0 * speed_y * (top_val + bottom_val - 2.0 * center)
    return jnp.stack([rate_mean, rate_x, rate_y], axis=1)


def reference(state, tangent, orient, walls):
    half_grid = NVX // 2
    weight = (5.0 / half_grid) ** 3
    block_count = 16
    block_size = NV // block_count
    point_count = 4 * CROSSWISE_SLABS * STREAMWISE_SLABS
    slot_all = jnp.arange(NV, dtype=jnp.int32)
    state_blocks = state.reshape(block_count, block_size, 3, CROSSWISE_SLABS, STREAMWISE_SLABS)
    tangent_blocks = tangent.reshape(block_count, block_size, 3, CROSSWISE_SLABS, STREAMWISE_SLABS)
    orient_blocks = orient.reshape(block_count, block_size, 2)
    slot_blocks = slot_all.reshape(block_count, block_size)

    def add_moments(running, pieces):
        state_blk, tangent_blk, orient_blk, slot_blk = pieces
        vel_x, vel_y, molecular_grid_extent = velocities(slot_blk, orient_blk, half_grid)
        moment_rows = moment_table(vel_x, vel_y, molecular_grid_extent, weight)
        part_state = jnp.dot(moment_rows, gauss_points(state_blk).reshape(block_size, point_count),
                             precision=lax.Precision.HIGHEST, preferred_element_type=jnp.float32)
        part_tangent = jnp.dot(moment_rows, gauss_points(tangent_blk).reshape(block_size, point_count),
                               precision=lax.Precision.HIGHEST, preferred_element_type=jnp.float32)
        return running + jnp.concatenate([part_state, part_tangent], axis=0), None

    moments, _ = lax.scan(add_moments, jnp.zeros((20, point_count), jnp.float32),
                          (state_blocks, tangent_blocks, orient_blocks, slot_blocks))
    params = gauss_params(moments)
    floor_flag = walls[0].astype(jnp.float32)
    roof_flag = walls[1].astype(jnp.float32)

    def one_block(pieces):
        tangent_blk, orient_blk, slot_blk = pieces
        vel_x, vel_y, molecular_grid_extent = velocities(slot_blk, orient_blk, half_grid)
        center, grad_x, grad_y = tangent_blk[:, 0], tangent_blk[:, 1], tangent_blk[:, 2]
        left_in = (jnp.roll(center + grad_x, 1, axis=2), jnp.roll(grad_y, 1, axis=2))
        right_in = (jnp.roll(center - grad_x, -1, axis=2), jnp.roll(grad_y, -1, axis=2))
        below_in = (jnp.concatenate([floor_flag * partner(center - grad_y)[:, :1], (center + grad_y)[:, :-1]], axis=1),
                    jnp.concatenate([floor_flag * partner(grad_x)[:, :1], grad_x[:, :-1]], axis=1))
        above_in = (jnp.concatenate([(center - grad_y)[:, 1:], roof_flag * partner(center + grad_y)[:, -1:]], axis=1),
                    jnp.concatenate([grad_x[:, 1:], roof_flag * partner(grad_x)[:, -1:]], axis=1))
        advected = transport(tangent_blk, orient_blk, vel_x, vel_y, left_in, right_in, below_in, above_in)
        gauss_delta = gauss_tangent(vel_x, vel_y, molecular_grid_extent, params).reshape(block_size, 4, CROSSWISE_SLABS, STREAMWISE_SLABS)
        return advected + COLLIDE * (tangent_blk - project_points(gauss_delta))

    result = lax.map(one_block, (tangent_blocks, orient_blocks, slot_blocks))
    return result.reshape(NV, 3, CROSSWISE_SLABS, STREAMWISE_SLABS)
```

```python
import functools
import math

import jax
import jax.numpy as jnp
from jax import lax
from jax.experimental import pallas as pl
from jax.experimental.pallas import tpu as pltpu
from jax.sharding import PartitionSpec as P

NVX = 20
GAUSS = 0.5773502691896258
XI_SIGNS = (-1.0, -1.0, 1.0, 1.0)
ETA_SIGNS = (-1.0, 1.0, -1.0, 1.0)
DUOS = ((0, 0), (1, 1), (2, 2), (0, 1), (0, 2), (1, 2))
LOG_TWO_PI = math.log(2.0 * math.pi)
LOG2E = 1.0 / math.log(2.0)
HALF = NVX // 2
SPACING = 5.0 / HALF
UNIT = 0.5 * SPACING
FEATS = 16
SUB = 8
LANES = 128
CHUNK = 256
F32 = jnp.float32
BF16 = jnp.bfloat16
VMEM_LIMIT = 56 * 1024 * 1024


def roundup(value, unit):
    return -(-value // unit) * unit


def for_blocks(count, body, unroll):
    whole = count // SUB
    rounds = whole // unroll

    def step(i, carry):
        for k in range(unroll):
            body(pl.multiple_of((i * unroll + k) * SUB, SUB))
        return carry

    if rounds:
        lax.fori_loop(0, rounds, step, 0)
    for k in range(rounds * unroll, whole):
        body(k * SUB)
    if count % SUB:
        body(count - SUB)


def swap_pairs(value, low):
    return jnp.where(low, pltpu.roll(value, SUB - 2, 0), pltpu.roll(value, 2, 0))


def iota(shape, dim):
    return lax.broadcasted_iota(jnp.int32, shape, dim)


def towards():
    return jnp.where(lax.axis_index("gy") == 0, 1, -1)


def fill_features(feat, orient_ref, count):
    feat[...] = jnp.zeros(feat.shape, F32)
    slot = (iota((1, count), 1) + lax.axis_index("vert") * count).astype(F32)
    jz = jnp.floor((slot + 0.5) * (1.0 / (4 * HALF * HALF)))
    slot = slot - jz * (4.0 * HALF * HALF)
    mx = jnp.floor((slot + 0.5) * (1.0 / (4 * HALF)))
    slot = slot - mx * (4.0 * HALF)
    my = jnp.floor((slot + 0.5) * 0.25)
    sx = (2 * orient_ref[0:1, :] - 1).astype(F32)
    sy = (2 * orient_ref[1:2, :] - 1).astype(F32)
    ox = sx * (2.0 * mx + 1.0)
    oy = sy * (2.0 * my + 1.0)
    oz = 2.0 * jz - (2.0 * HALF - 1.0)
    cross = (ox * oy, ox * oz, oy * oz)
    high = [jnp.floor(c * 0.0625) * 16.0 for c in cross]
    low = [c - h for c, h in zip(cross, high)]
    rows = [jnp.ones_like(ox), ox, oy, oz, mx * (mx + 1.0), my * (my + 1.0), 0.25 * (oz * oz - 1.0)]
    rows = rows + high + low + [sx, sy, 2.0 * my + 1.0]
    for k, row in enumerate(rows):
        feat[k : k + 1, 0:count] = row


def spread_table(columns, step):
    rows = iota((LANES, LANES * len(columns)), 0)
    blocks = iota((LANES, LANES * len(columns)), 1) // LANES
    out = jnp.zeros(rows.shape, F32)
    for j, (row, scale) in enumerate(columns):
        out = jnp.where((rows == row) & (blocks == j), scale, out)
    return out.astype(BF16)


def pieces(value):
    high = value.astype(BF16)
    rest = value - high.astype(F32)
    mid = rest.astype(BF16)
    low = (rest - mid.astype(F32)).astype(BF16)
    return high, mid, low


def dot(left, right):
    return jnp.dot(left, right, preferred_element_type=F32)


def pre_kernel(count, rows, orient_ref, tan_hbm, st_hbm, ysend, xsend, mom, tab, feat, wide, edge, tan_v, st_v, sems):
    comps = 3 * rows
    padded = feat.shape[1]
    starts = list(range(0, padded, CHUNK))
    copies = []
    for a, (src, dst) in enumerate(((tan_hbm, tan_v), (st_hbm, st_v))):
        for j, start in enumerate(starts):
            size = min(CHUNK, count - start) * comps
            part = pl.ds(start * comps, size)
            copies.append(pltpu.make_async_copy(src.at[part], dst.at[part], sems.at[a * len(starts) + j]))
    for copy in copies:
        copy.start()
    tail = (padded - count) * comps
    for buf in (tan_v, st_v):
        if tail:
            buf[pl.ds(count * comps, tail), :] = jnp.zeros((tail, LANES), F32)
    edge[...] = jnp.zeros(edge.shape, F32)
    fill_features(feat, orient_ref, count)
    table = feat[...]
    spare = jnp.zeros((LANES - 3 * FEATS, padded), F32)
    flipped = jnp.concatenate([table, table, table, spare], axis=0).T.astype(BF16)
    tab[...] = flipped
    away = towards()
    scale = away.astype(F32)
    wide[...] = dot(flipped, spread_table([(13, 1.0), (14, 1.0)], 1))
    face = jnp.where(away == 1, rows - 1, 0)
    sub = iota((SUB, LANES), 0)
    low = sub % 4 < 2
    lane = iota((SUB, LANES), 1)
    for copy in copies[: len(starts)]:
        copy.wait()

    def pack(start):
        at = lambda comp, row: tan_v[pl.ds(start * comps + comp * rows + row, SUB, stride=comps), :]
        sx = wide[pl.ds(start, SUB), 0:LANES]
        sy = wide[pl.ds(start, SUB), LANES : 2 * LANES]
        center, grad_x, grad_y = at(0, face), at(1, face), at(2, face)
        out_y = center + sy * grad_y
        own = jnp.where(low, out_y, grad_x)
        other = jnp.where(low, grad_x, out_y)
        ysend[pl.ds(start, SUB), :] = jnp.where(sy * scale > 0.0, own, swap_pairs(other, low))
        right = sx > 0.0
        acc = jnp.zeros((SUB, LANES), F32)
        for row in range(rows):
            slope = at(2, row)
            value = at(0, row) + sx * at(1, row)
            for j, piece in ((2 * row, value), (2 * row + 1, slope)):
                here = jnp.where(right, pltpu.roll(piece, 1 + j, 1), pltpu.roll(piece, j, 1) if j else piece)
                acc = jnp.where(lane == j, here, acc)
        edge[pl.ds(start, SUB), :] = acc

    for_blocks(count, pack, 5)
    xsend[...] = edge[...].T[0 : xsend.shape[0], :]
    table = table.astype(BF16)
    for a, buf in enumerate((tan_v, st_v)):
        if a:
            for copy in copies[len(starts) :]:
                copy.wait()
        for c in range(comps):
            total = jnp.zeros((FEATS, LANES), F32)
            for start in starts:
                size = min(CHUNK, padded - start)
                data = buf[pl.ds(start * comps + c, size, stride=comps), :]
                high = data.astype(BF16)
                rest = (data - high.astype(F32)).astype(BF16)
                part = table[:, start : start + size]
                total = total + dot(part, high) + dot(part, rest)
            ones = total[0:1]
            squares = 4.0 * total[4:7] + ones
            cross = total[7:10] + total[10:13]
            slot = (1 - a) * comps + c
            mom[pl.ds(slot * 8, 4), :] = total[0:4]
            mom[pl.ds(slot * 8 + 4, 3), :] = squares
            mom[pl.ds(slot * 8 + 7, 1), :] = cross[0:1]
            mom[pl.ds(2 * comps * 8 + slot * 2, 2), :] = cross[1:3]


def transport_kernel(count, rows, cols, single, *refs):
    orient_ref, tan_v, tab, walls, behind = refs[:5]
    ahead = behind if single else refs[5]
    adv, wide = refs[-2:]
    comps = 3 * rows
    padded = tab.shape[0]
    away = towards()
    scale = away.astype(F32)
    right_row = jnp.concatenate([orient_ref[0:1, :], jnp.zeros((1, padded - count), jnp.int32)], axis=1) == 1
    arrived = jnp.where(right_row, behind[...], ahead[...])
    spare = jnp.zeros((LANES - 3 * SUB, padded), F32)
    parts = [piece.astype(F32) for piece in pieces(arrived)]
    edges = jnp.concatenate(parts + [spare], axis=0).T.astype(BF16)
    cols_w = [(1, UNIT), (2, UNIT), (15, UNIT), (13, 1.0), (14, scale)]
    wide[:, 0 : 5 * LANES] = dot(tab[...], spread_table(cols_w, 1))
    r = iota((LANES, LANES * 2 * rows), 0)
    b = iota((LANES, LANES * 2 * rows), 1) // LANES
    pick = jnp.where((r % SUB == b) & (r < 3 * SUB), 1.0, 0.0).astype(BF16)
    wide[:, 5 * LANES : (5 + 2 * rows) * LANES] = dot(edges, pick)
    sub = iota((SUB, LANES), 0)
    low = sub % 4 < 2
    lane = iota((SUB, LANES), 1)
    ends = jnp.where(lane == cols - 1, 1.0, 0.0) - jnp.where(lane == 0, 1.0, 0.0)
    wall_row = jnp.where(away == 1, walls[0:1, :], walls[1:2, :]).astype(F32)
    wall = jnp.broadcast_to(wall_row, (SUB, LANES))
    order = [jnp.where(away == 1, k, rows - 1 - k) for k in range(rows)]

    def block(start):
        at = lambda comp, row: tan_v[pl.ds(start * comps + comp * rows + row, SUB, stride=comps), :]
        col = lambda j: wide[pl.ds(start, SUB), j * LANES : (j + 1) * LANES]
        vx, vy, ay, sx, toward_sign = (col(j) for j in range(5))
        ax = vx * sx
        sy = toward_sign * scale
        right = sx > 0.0
        toward = toward_sign > 0.0
        outgoing = sx * ends > 0.0
        center = [at(0, order[k]) for k in range(rows)]
        grad_x = [at(1, order[k]) for k in range(rows)]
        grad_y = [at(2, order[k]) for k in range(rows)]
        out_y = [c + sy * g for c, g in zip(center, grad_y)]
        for k in range(rows):
            ecol = lambda j: wide[pl.ds(start, SUB), pl.ds(pl.multiple_of((5 + 2 * order[k] + j) * LANES, LANES), LANES)]
            out_x = center[k] + sx * grad_x[k]

            def inflow(piece, received):
                mixed = jnp.where(outgoing, received, piece)
                return jnp.where(right, pltpu.roll(mixed, 1, 1), pltpu.roll(mixed, cols - 1, 1))

            in_x = inflow(out_x, ecol(0))
            in_xs = inflow(grad_y[k], ecol(1))
            if k == 0:
                near_v = wall * swap_pairs(out_y[0], low)
                near_s = wall * swap_pairs(grad_x[0], low)
            else:
                near_v, near_s = out_y[k - 1], grad_x[k - 1]
            if k == rows - 1:
                far_v, far_s = jnp.zeros_like(near_v), jnp.zeros_like(near_s)
            else:
                far_v, far_s = out_y[k + 1], grad_x[k + 1]
            in_y = jnp.where(toward, near_v, far_v)
            in_ys = jnp.where(toward, near_s, far_s)
            twice = 2.0 * center[k]
            mean = ax * (out_x - in_x) + ay * (out_y[k] - in_y) + twice
            rate_x = 3.0 * vx * (out_x + in_x - twice) + ay * (grad_x[k] - in_ys) + 2.0 * grad_x[k]
            rate_y = ax * (grad_y[k] - in_xs) + 3.0 * vy * (out_y[k] + in_y - twice) + 2.0 * grad_y[k]
            for comp, value in enumerate((mean, rate_x, rate_y)):
                adv[pl.ds(start * comps + comp * rows + order[k], SUB, stride=comps), :] = value

    for_blocks(count, block, 2)


def sym(entries):
    grid = [[None] * 3 for _ in range(3)]
    for k, (i, j) in enumerate(DUOS):
        grid[i][j] = entries[k]
        grid[j][i] = entries[k]
    return grid


def point_params(moments):
    density = moments[0]
    inv_density = 1.0 / density
    u = [moments[1 + i] * inv_density for i in range(3)]
    second = [moments[4 + k] for k in range(6)]
    theta = [second[k] * inv_density - u[i] * u[j] for k, (i, j) in enumerate(DUOS)]
    temp = (theta[0] + theta[1] + theta[2]) / 3.0
    tensor = [(1.5 * temp if i == j else 0.0) - 0.5 * theta[k] for k, (i, j) in enumerate(DUOS)]
    t = sym(tensor)
    cof = [
        t[1][1] * t[2][2] - t[1][2] * t[1][2],
        t[0][0] * t[2][2] - t[0][2] * t[0][2],
        t[0][0] * t[1][1] - t[0][1] * t[0][1],
        t[0][2] * t[1][2] - t[0][1] * t[2][2],
        t[0][1] * t[1][2] - t[0][2] * t[1][1],
        t[0][1] * t[0][2] - t[0][0] * t[1][2],
    ]
    det = t[0][0] * cof[0] + t[0][1] * cof[3] + t[0][2] * cof[4]
    inv_det = 1.0 / det
    inverse = [entry * inv_det for entry in cof]
    log_pre = jnp.log(density) - 1.5 * LOG_TWO_PI - 0.5 * jnp.log(det)
    drho = moments[10]
    du = [(moments[11 + i] - u[i] * drho) * inv_density for i in range(3)]
    ratio = drho * inv_density
    dtheta = [
        moments[14 + k] * inv_density - second[k] * inv_density * ratio - (du[i] * u[j] + u[i] * du[j])
        for k, (i, j) in enumerate(DUOS)
    ]
    dtemp = (dtheta[0] + dtheta[1] + dtheta[2]) / 3.0
    dtensor = [(1.5 * dtemp if i == j else 0.0) - 0.5 * dtheta[k] for k, (i, j) in enumerate(DUOS)]
    a, d = sym(inverse), sym(dtensor)
    trace = sum(a[i][j] * d[j][i] for i in range(3) for j in range(3))
    shift = ratio - 0.5 * trace
    w = [a[i][0] * du[0] + a[i][1] * du[1] + a[i][2] * du[2] for i in range(3)]
    ad = [[a[i][0] * d[0][j] + a[i][1] * d[1][j] + a[i][2] * d[2][j] for j in range(3)] for i in range(3)]
    curve = [ad[i][0] * a[0][j] + ad[i][1] * a[1][j] + ad[i][2] * a[2][j] for i, j in DUOS]
    return u, inverse, log_pre, shift, w, curve


def feature_coefs(const, linear, quad):
    square = [UNIT * UNIT * quad[k] for k in range(6)]
    const = const + square[0] + square[1] + square[2]
    return [const] + [UNIT * l for l in linear] + [4.0 * s for s in square[:3]] + square[3:] + square[3:]


def collide_kernel(count, rows, mom, tab, adv, out, raw, turn, coef, power):
    comps = 3 * rows
    spots = 4 * rows
    weight = SPACING**3
    scales = [weight] + [weight * UNIT] * 3 + [weight * UNIT * UNIT] * 4
    row_scale = jnp.zeros((SUB, LANES), F32)
    sub = iota((SUB, LANES), 0)
    for k, s in enumerate(scales):
        row_scale = jnp.where(sub == k, s, row_scale)
    for a in range(2):
        for row in range(rows):
            first = [row_scale * mom[pl.ds((a * comps + c * rows + row) * 8, 8), :] for c in range(3)]
            last = [
                (weight * UNIT * UNIT) * mom[pl.ds(2 * comps * 8 + (a * comps + c * rows + row) * 2, 2), :]
                for c in range(3)
            ]
            for q in range(4):
                mix = lambda v: v[0] + (XI_SIGNS[q] * GAUSS) * v[1] + (ETA_SIGNS[q] * GAUSS) * v[2]
                base = (q * rows + row) * 24 + a * 10
                raw[pl.ds(base, 8), :] = mix(first)
                raw[pl.ds(base + 8, 2), :] = mix(last)
    moments = [raw[pl.ds(k, spots, stride=24), :] for k in range(20)]
    u, inverse, log_pre, shift, w, curve = point_params(moments)
    a, b = sym(inverse), sym(curve)
    au = [a[i][0] * u[0] + a[i][1] * u[1] + a[i][2] * u[2] for i in range(3)]
    bu = [b[i][0] * u[0] + b[i][1] * u[1] + b[i][2] * u[2] for i in range(3)]
    uau = u[0] * au[0] + u[1] * au[1] + u[2] * au[2]
    ubu = u[0] * bu[0] + u[1] * bu[1] + u[2] * bu[2]
    uw = u[0] * w[0] + u[1] * w[1] + u[2] * w[2]
    half = lambda m, k: (0.5 if k < 3 else 1.0) * m[k]
    expo = feature_coefs(
        LOG2E * (log_pre - 0.5 * uau),
        [LOG2E * v for v in au],
        [-LOG2E * half(inverse, k) for k in range(6)],
    )
    poly = feature_coefs(
        0.5 * (shift - uw + 0.5 * ubu),
        [0.5 * (w[i] - bu[i]) for i in range(3)],
        [0.5 * half(curve, k) for k in range(6)],
    )
    coef[...] = jnp.zeros(coef.shape, BF16)
    for p, entries in enumerate((expo, poly)):
        turn[...] = jnp.zeros(turn.shape, F32)
        for k, entry in enumerate(entries):
            turn[pl.ds(k * spots, spots), :] = entry
        for s in range(spots):
            lanes = pl.ds((p * spots + s) * LANES, LANES)
            for j, piece in enumerate(pieces(turn[pl.ds(s, FEATS, stride=spots), :])):
                coef[pl.ds(j * FEATS, FEATS), lanes] = piece
    root3 = 3.0 * GAUSS
    for start in range(0, count, CHUNK):
        size = min(CHUNK, count - start)
        power[...] = dot(tab[pl.ds(start, CHUNK), :], coef[...])

        def block(local):
            first = (start + local) * comps
            for row in range(rows):
                gd = []
                for q in range(4):
                    lane = (q * rows + row) * LANES
                    expo = power[pl.ds(local, SUB), lane : lane + LANES]
                    factor = power[pl.ds(local, SUB), spots * LANES + lane : spots * LANES + lane + LANES]
                    gd.append(jnp.exp2(expo) * factor)
                back, front = gd[0] + gd[1], gd[2] + gd[3]
                collided = (back + front, root3 * (front - back), root3 * ((gd[1] - gd[0]) + (gd[3] - gd[2])))
                for comp, value in enumerate(collided):
                    where = pl.ds(first + comp * rows + row, SUB, stride=comps)
                    out[where, :] = adv[where, :] - value

        for_blocks(size, block, 2)


def face_kernel(count, rows, col, tab, yrecv, out_hbm, out_v, wide, sems):
    comps = 3 * rows
    away = towards()
    scale = away.astype(F32)
    face = jnp.where(away == 1, rows - 1, 0)
    wide[...] = dot(tab[...], spread_table([(15, UNIT), (14, scale)], 1))
    low = iota((SUB, LANES), 0) % 4 < 2
    copies = []
    for j, start in enumerate(range(0, count, CHUNK)):
        size = min(CHUNK, count - start)
        part = pl.ds(start * comps, size * comps)
        out_v[part, :] = col[part, :]

        def block(local):
            at = start + local
            data = yrecv[pl.ds(at, SUB), :]
            turned = swap_pairs(data, low)
            speed = wide[pl.ds(at, SUB), 0:LANES]
            sign = wide[pl.ds(at, SUB), LANES : 2 * LANES]
            speed = jnp.where(sign < 0.0, speed, 0.0)
            value = speed * jnp.where(low, data, turned)
            slope = speed * jnp.where(low, turned, data)
            for comp, term in enumerate((value, slope, (3.0 * scale) * value)):
                where = pl.ds(at * comps + comp * rows + face, SUB, stride=comps)
                out_v[where, :] = col[where, :] - term

        for_blocks(size, block, 4)
        copies.append(pltpu.make_async_copy(out_v.at[part], out_hbm.at[part], sems.at[j]))
        copies[-1].start()
    for copy in copies:
        copy.wait()


def call(kernel, out_shape, scratch, ins, outs, name):
    return pl.pallas_call(
        kernel,
        out_shape=out_shape,
        in_specs=[pl.BlockSpec(memory_space=m) for m in ins],
        out_specs=jax.tree.map(lambda m: pl.BlockSpec(memory_space=m), outs),
        scratch_shapes=scratch,
        compiler_params=pltpu.CompilerParams(vmem_limit_bytes=VMEM_LIMIT),
        name=name,
    )


def exchange(value, axis, by):
    devices = lax.axis_size(axis)
    return lax.ppermute(value, axis, [(i, (i + by) % devices) for i in range(devices)])


def sum_over(value, axis):
    devices = lax.axis_size(axis)
    step = 1
    while step < devices:
        value = value + lax.ppermute(value, axis, [(i, i ^ step) for i in range(devices)])
        step *= 2
    return value


def shards(state, tangent, orient, walls):
    count, _, rows, cols = state.shape
    comps = 3 * rows
    total_rows = count * comps
    padded = roundup(count, CHUNK)
    chunks = padded // CHUNK
    st = state.reshape(total_rows, cols)
    tn = tangent.reshape(total_rows, cols)
    signs = orient.T
    vm, hbm = pltpu.VMEM, pl.ANY
    shape = jax.ShapeDtypeStruct
    ysend, xsend, mom, tab = call(
        functools.partial(pre_kernel, count, rows),
        (
            shape((count, cols), F32),
            shape((SUB, padded), F32),
            shape((2 * comps * 10, cols), F32),
            shape((padded, LANES), BF16),
        ),
        [
            pltpu.VMEM((FEATS, padded), F32),
            pltpu.VMEM((padded, 2 * LANES), F32),
            pltpu.VMEM((padded, LANES), F32),
            pltpu.VMEM((padded * comps, cols), F32),
            pltpu.VMEM((padded * comps, cols), F32),
            pltpu.SemaphoreType.DMA((2 * chunks,)),
        ],
        (vm, hbm, hbm),
        (vm, vm, vm, vm),
        "pack_and_moments",
    )(signs, tn, st)
    yrecv = lax.ppermute(ysend, "gy", [(0, 1), (1, 0)])
    single = lax.axis_size("gx") == 2
    behind = exchange(xsend, "gx", 1)
    edges = (behind,) if single else (behind, exchange(xsend, "gx", -1))
    mom = sum_over(mom, "vert")
    adv = call(
        functools.partial(transport_kernel, count, rows, cols, single),
        shape((total_rows, cols), F32),
        [pltpu.VMEM((padded, (5 + 2 * rows) * LANES), F32)],
        (vm,) * (4 + len(edges)),
        vm,
        "transport",
    )(signs, tn, tab, walls, *edges)
    col = call(
        functools.partial(collide_kernel, count, rows),
        shape((total_rows, cols), F32),
        [
            pltpu.VMEM((4 * rows * 24, LANES), F32),
            pltpu.VMEM((FEATS * 4 * rows, LANES), F32),
            pltpu.VMEM((LANES, 8 * rows * LANES), BF16),
            pltpu.VMEM((CHUNK, 8 * rows * LANES), F32),
        ],
        (vm, vm, vm),
        vm,
        "collide",
    )(mom, tab, adv)
    out = call(
        functools.partial(face_kernel, count, rows),
        shape((total_rows, cols), F32),
        [
            pltpu.VMEM((total_rows, cols), F32),
            pltpu.VMEM((padded, 2 * LANES), F32),
            pltpu.SemaphoreType.DMA((chunks,)),
        ],
        (vm, vm, vm),
        hbm,
        "faces",
    )(col, tab, yrecv)
    return out.reshape(state.shape)


def solution(mesh):
    placed = (
        P("vert", None, "gy", "gx"),
        P("vert", None, "gy", "gx"),
        P("vert", None),
        P(None, "gx"),
    )
    return jax.shard_map(
        shards, mesh=mesh, in_specs=placed, out_specs=P("vert", None, "gy", "gx"), check_vma=False
    )
```

```python
import functools
import math

import jax
import jax.numpy as jnp
from jax import lax
from jax.experimental import pallas as pl
from jax.experimental.pallas import tpu as pltpu
from jax.sharding import PartitionSpec as P

NVX = 20
GAUSS = 0.5773502691896258
XI_SIGNS = (-1.0, -1.0, 1.0, 1.0)
ETA_SIGNS = (-1.0, 1.0, -1.0, 1.0)
DUOS = ((0, 0), (1, 1), (2, 2), (0, 1), (0, 2), (1, 2))
LOG_TWO_PI = math.log(2.0 * math.pi)
LOG2E = 1.0 / math.log(2.0)
HALF = NVX // 2
SPACING = 5.0 / HALF
UNIT = 0.5 * SPACING
FEATS = 16
SUB = 8
LANES = 128
CHUNK = 256
U_PACK, U_TRANS, U_COLL, U_FACE = 25, 16, 16, 32
F32 = jnp.float32
BF16 = jnp.bfloat16
VMEM_LIMIT = 16 * 1024 * 1024


def roundup(value, unit):
    return -(-value // unit) * unit


def for_blocks(count, body, unroll):
    whole = count // SUB
    rounds = whole // unroll

    def group(firsts):
        for ref, where, value in [store for first in firsts for store in body(first)]:
            ref[where] = value

    def step(i, carry):
        group([pl.multiple_of((i * unroll + k) * SUB, SUB) for k in range(unroll)])
        return carry

    if rounds:
        lax.fori_loop(0, rounds, step, 0)
    left = [k * SUB for k in range(rounds * unroll, whole)]
    if left:
        group(left)
    if count % SUB:
        group([count - SUB])


def swap_pairs(value, low):
    return jnp.where(low, pltpu.roll(value, SUB - 2, 0), pltpu.roll(value, 2, 0))


def iota(shape, dim):
    return lax.broadcasted_iota(jnp.int32, shape, dim)


def towards():
    return jnp.where(lax.axis_index("gy") == 0, 1, -1)


def fill_features(feat, orient_ref, count):
    feat[...] = jnp.zeros(feat.shape, F32)
    slot = (iota((1, count), 1) + lax.axis_index("vert") * count).astype(F32)
    jz = jnp.floor((slot + 0.5) * (1.0 / (4 * HALF * HALF)))
    slot = slot - jz * (4.0 * HALF * HALF)
    mx = jnp.floor((slot + 0.5) * (1.0 / (4 * HALF)))
    slot = slot - mx * (4.0 * HALF)
    my = jnp.floor((slot + 0.5) * 0.25)
    sx = (2 * orient_ref[0:1, :] - 1).astype(F32)
    sy = (2 * orient_ref[1:2, :] - 1).astype(F32)
    ox = sx * (2.0 * mx + 1.0)
    oy = sy * (2.0 * my + 1.0)
    oz = 2.0 * jz - (2.0 * HALF - 1.0)
    cross = (ox * oy, ox * oz, oy * oz)
    high = [jnp.floor(c * 0.0625) * 16.0 for c in cross]
    low = [c - h for c, h in zip(cross, high)]
    rows = [jnp.ones_like(ox), ox, oy, oz, mx * (mx + 1.0), my * (my + 1.0), 0.25 * (oz * oz - 1.0)]
    rows = rows + high + low + [sx, sy, 2.0 * my + 1.0]
    for k, row in enumerate(rows):
        feat[k : k + 1, 0:count] = row


def spread_table(columns, step):
    rows = iota((LANES, LANES * len(columns)), 0)
    blocks = iota((LANES, LANES * len(columns)), 1) // LANES
    out = jnp.zeros(rows.shape, F32)
    for j, (row, scale) in enumerate(columns):
        out = jnp.where((rows == row) & (blocks == j), scale, out)
    return out.astype(BF16)


def pieces(value):
    high = value.astype(BF16)
    rest = value - high.astype(F32)
    mid = rest.astype(BF16)
    low = (rest - mid.astype(F32)).astype(BF16)
    return high, mid, low


def dot(left, right):
    return jnp.dot(left, right, preferred_element_type=F32)


def pre_kernel(count, rows, orient_hbm, tan_hbm, st_hbm, ysend, xsend, mom, tab, tan_v, orient_ref, feat, wide, edge, st_v, sems):
    comps = 3 * rows
    padded = feat.shape[1]
    starts = list(range(0, padded, CHUNK))
    copies = []
    for a, (src, dst) in enumerate(((tan_hbm, tan_v), (st_hbm, st_v))):
        for j, start in enumerate(starts):
            size = min(CHUNK, count - start) * comps
            part = pl.ds(start * comps, size)
            copies.append(pltpu.make_async_copy(src.at[part], dst.at[part], sems.at[a * len(starts) + j]))
    signs = pltpu.make_async_copy(orient_hbm, orient_ref, sems.at[2 * len(starts)])
    signs.start()
    for copy in copies:
        copy.start()
    tail = (padded - count) * comps
    for buf in (tan_v, st_v):
        if tail:
            buf[pl.ds(count * comps, tail), :] = jnp.zeros((tail, LANES), F32)
    edge[...] = jnp.zeros(edge.shape, F32)
    signs.wait()
    fill_features(feat, orient_ref, count)
    table = feat[...]
    spare = jnp.zeros((LANES - 3 * FEATS, padded), F32)
    flipped = jnp.concatenate([table, table, table, spare], axis=0).T.astype(BF16)
    tab[...] = flipped
    away = towards()
    scale = away.astype(F32)
    wide[...] = dot(flipped, spread_table([(13, 1.0), (14, 1.0)], 1))
    face = jnp.where(away == 1, rows - 1, 0)
    sub = iota((SUB, LANES), 0)
    low = sub % 4 < 2
    lane = iota((SUB, LANES), 1)
    for copy in copies[: len(starts)]:
        copy.wait()

    def pack(start):
        at = lambda comp, row: tan_v[pl.ds(start * comps + comp * rows + row, SUB, stride=comps), :]
        sx = wide[pl.ds(start, SUB), 0:LANES]
        sy = wide[pl.ds(start, SUB), LANES : 2 * LANES]
        center, grad_x, grad_y = at(0, face), at(1, face), at(2, face)
        out_y = center + sy * grad_y
        own = jnp.where(low, out_y, grad_x)
        other = jnp.where(low, grad_x, out_y)
        packed = jnp.where(sy * scale > 0.0, own, swap_pairs(other, low))
        right = sx > 0.0
        acc = jnp.zeros((SUB, LANES), F32)
        for row in range(rows):
            slope = at(2, row)
            value = at(0, row) + sx * at(1, row)
            for j, piece in ((2 * row, value), (2 * row + 1, slope)):
                here = jnp.where(right, pltpu.roll(piece, 1 + j, 1), pltpu.roll(piece, j, 1) if j else piece)
                acc = jnp.where(lane == j, here, acc)
        where = (pl.ds(start, SUB), slice(None))
        return [(ysend, where, packed), (edge, where, acc)]

    for_blocks(count, pack, U_PACK)
    xsend[...] = edge[...].T[0 : xsend.shape[0], :]
    table = table.astype(BF16)
    for a, buf in enumerate((tan_v, st_v)):
        if a:
            for copy in copies[len(starts) :]:
                copy.wait()
        for c in range(comps):
            total = jnp.zeros((FEATS, LANES), F32)
            for start in starts:
                size = min(CHUNK, padded - start)
                data = buf[pl.ds(start * comps + c, size, stride=comps), :]
                high = data.astype(BF16)
                rest = (data - high.astype(F32)).astype(BF16)
                part = table[:, start : start + size]
                total = total + dot(part, high) + dot(part, rest)
            ones = total[0:1]
            squares = 4.0 * total[4:7] + ones
            cross = total[7:10] + total[10:13]
            slot = (1 - a) * comps + c
            mom[pl.ds(slot * 8, 4), :] = total[0:4]
            mom[pl.ds(slot * 8 + 4, 3), :] = squares
            mom[pl.ds(slot * 8 + 7, 1), :] = cross[0:1]
            mom[pl.ds(2 * comps * 8 + slot * 2, 2), :] = cross[1:3]


def transport_kernel(count, rows, cols, single, *refs):
    tan_v, tab, walls, behind = refs[:4]
    adv, wide = refs[-2:]
    comps = 3 * rows
    padded = tab.shape[0]
    away = towards()
    scale = away.astype(F32)
    arrived = behind[...]
    if not single:
        ahead, signs = refs[4:6]
        spare = [jnp.zeros((1, padded - count), jnp.int32)] if padded > count else []
        right_row = jnp.concatenate([signs[0:1, :]] + spare, axis=1) == 1
        arrived = jnp.where(right_row, arrived, ahead[...])
    spare = jnp.zeros((LANES - 3 * SUB, padded), F32)
    parts = [piece.astype(F32) for piece in pieces(arrived)]
    edges = jnp.concatenate(parts + [spare], axis=0).T.astype(BF16)
    cols_w = [(1, UNIT), (2, UNIT), (15, UNIT), (13, 1.0), (14, scale)]
    wide[:, 0 : 5 * LANES] = dot(tab[...], spread_table(cols_w, 1))
    r = iota((LANES, LANES * 2 * rows), 0)
    b = iota((LANES, LANES * 2 * rows), 1) // LANES
    pick = jnp.where((r % SUB == b) & (r < 3 * SUB), 1.0, 0.0).astype(BF16)
    wide[:, 5 * LANES : (5 + 2 * rows) * LANES] = dot(edges, pick)
    sub = iota((SUB, LANES), 0)
    low = sub % 4 < 2
    lane = iota((SUB, LANES), 1)
    ends = jnp.where(lane == cols - 1, 1.0, 0.0) - jnp.where(lane == 0, 1.0, 0.0)
    wall_row = jnp.where(away == 1, walls[0:1, :], walls[1:2, :]).astype(F32)
    wall = jnp.broadcast_to(wall_row, (SUB, LANES))
    order = [jnp.where(away == 1, k, rows - 1 - k) for k in range(rows)]

    def block(start):
        at = lambda comp, row: tan_v[pl.ds(start * comps + comp * rows + row, SUB, stride=comps), :]
        col = lambda j: wide[pl.ds(start, SUB), j * LANES : (j + 1) * LANES]
        vx, vy, ay, sx, toward_sign = (col(j) for j in range(5))
        ax = vx * sx
        sy = toward_sign * scale
        right = sx > 0.0
        toward = toward_sign > 0.0
        outgoing = sx * ends > 0.0
        center = [at(0, order[k]) for k in range(rows)]
        grad_x = [at(1, order[k]) for k in range(rows)]
        grad_y = [at(2, order[k]) for k in range(rows)]
        out_y = [c + sy * g for c, g in zip(center, grad_y)]
        stores = []
        for k in range(rows):
            ecol = lambda j: wide[pl.ds(start, SUB), pl.ds(pl.multiple_of((5 + 2 * order[k] + j) * LANES, LANES), LANES)]
            out_x = center[k] + sx * grad_x[k]

            def inflow(piece, received):
                mixed = jnp.where(outgoing, received, piece)
                return jnp.where(right, pltpu.roll(mixed, 1, 1), pltpu.roll(mixed, cols - 1, 1))

            in_x = inflow(out_x, ecol(0))
            in_xs = inflow(grad_y[k], ecol(1))
            if k == 0:
                near_v = wall * swap_pairs(out_y[0], low)
                near_s = wall * swap_pairs(grad_x[0], low)
            else:
                near_v, near_s = out_y[k - 1], grad_x[k - 1]
            if k == rows - 1:
                far_v, far_s = jnp.zeros_like(near_v), jnp.zeros_like(near_s)
            else:
                far_v, far_s = out_y[k + 1], grad_x[k + 1]
            in_y = jnp.where(toward, near_v, far_v)
            in_ys = jnp.where(toward, near_s, far_s)
            twice = 2.0 * center[k]
            mean = ax * (out_x - in_x) + ay * (out_y[k] - in_y) + twice
            rate_x = 3.0 * vx * (out_x + in_x - twice) + ay * (grad_x[k] - in_ys) + 2.0 * grad_x[k]
            rate_y = ax * (grad_y[k] - in_xs) + 3.0 * vy * (out_y[k] + in_y - twice) + 2.0 * grad_y[k]
            for comp, value in enumerate((mean, rate_x, rate_y)):
                where = pl.ds(start * comps + comp * rows + order[k], SUB, stride=comps)
                stores.append((adv, (where, slice(None)), value))
        return stores

    for_blocks(count, block, U_TRANS)


def sym(entries):
    grid = [[None] * 3 for _ in range(3)]
    for k, (i, j) in enumerate(DUOS):
        grid[i][j] = entries[k]
        grid[j][i] = entries[k]
    return grid


def point_params(moments):
    density = moments[0]
    inv_density = 1.0 / density
    u = [moments[1 + i] * inv_density for i in range(3)]
    second = [moments[4 + k] for k in range(6)]
    theta = [second[k] * inv_density - u[i] * u[j] for k, (i, j) in enumerate(DUOS)]
    temp = (theta[0] + theta[1] + theta[2]) / 3.0
    tensor = [(1.5 * temp if i == j else 0.0) - 0.5 * theta[k] for k, (i, j) in enumerate(DUOS)]
    t = sym(tensor)
    cof = [
        t[1][1] * t[2][2] - t[1][2] * t[1][2],
        t[0][0] * t[2][2] - t[0][2] * t[0][2],
        t[0][0] * t[1][1] - t[0][1] * t[0][1],
        t[0][2] * t[1][2] - t[0][1] * t[2][2],
        t[0][1] * t[1][2] - t[0][2] * t[1][1],
        t[0][1] * t[0][2] - t[0][0] * t[1][2],
    ]
    det = t[0][0] * cof[0] + t[0][1] * cof[3] + t[0][2] * cof[4]
    inv_det = 1.0 / det
    inverse = [entry * inv_det for entry in cof]
    log_pre = jnp.log(density) - 1.5 * LOG_TWO_PI - 0.5 * jnp.log(det)
    drho = moments[10]
    du = [(moments[11 + i] - u[i] * drho) * inv_density for i in range(3)]
    ratio = drho * inv_density
    dtheta = [
        moments[14 + k] * inv_density - second[k] * inv_density * ratio - (du[i] * u[j] + u[i] * du[j])
        for k, (i, j) in enumerate(DUOS)
    ]
    dtemp = (dtheta[0] + dtheta[1] + dtheta[2]) / 3.0
    dtensor = [(1.5 * dtemp if i == j else 0.0) - 0.5 * dtheta[k] for k, (i, j) in enumerate(DUOS)]
    a, d = sym(inverse), sym(dtensor)
    trace = sum(a[i][j] * d[j][i] for i in range(3) for j in range(3))
    shift = ratio - 0.5 * trace
    w = [a[i][0] * du[0] + a[i][1] * du[1] + a[i][2] * du[2] for i in range(3)]
    ad = [[a[i][0] * d[0][j] + a[i][1] * d[1][j] + a[i][2] * d[2][j] for j in range(3)] for i in range(3)]
    curve = [ad[i][0] * a[0][j] + ad[i][1] * a[1][j] + ad[i][2] * a[2][j] for i, j in DUOS]
    return u, inverse, log_pre, shift, w, curve


def feature_coefs(const, linear, quad):
    square = [UNIT * UNIT * quad[k] for k in range(6)]
    const = const + square[0] + square[1] + square[2]
    return [const] + [UNIT * l for l in linear] + [4.0 * s for s in square[:3]] + square[3:] + square[3:]


def collide_kernel(count, rows, mom, tab, adv, out, raw, turn, coef, power):
    comps = 3 * rows
    spots = 4 * rows
    weight = SPACING**3
    scales = [weight] + [weight * UNIT] * 3 + [weight * UNIT * UNIT] * 4
    row_scale = jnp.zeros((SUB, LANES), F32)
    sub = iota((SUB, LANES), 0)
    for k, s in enumerate(scales):
        row_scale = jnp.where(sub == k, s, row_scale)
    for a in range(2):
        for row in range(rows):
            first = [row_scale * mom[pl.ds((a * comps + c * rows + row) * 8, 8), :] for c in range(3)]
            last = [
                (weight * UNIT * UNIT) * mom[pl.ds(2 * comps * 8 + (a * comps + c * rows + row) * 2, 2), :]
                for c in range(3)
            ]
            for q in range(4):
                mix = lambda v: v[0] + (XI_SIGNS[q] * GAUSS) * v[1] + (ETA_SIGNS[q] * GAUSS) * v[2]
                base = (q * rows + row) * 24 + a * 10
                raw[pl.ds(base, 8), :] = mix(first)
                raw[pl.ds(base + 8, 2), :] = mix(last)
    moments = [raw[pl.ds(k, spots, stride=24), :] for k in range(20)]
    u, inverse, log_pre, shift, w, curve = point_params(moments)
    a, b = sym(inverse), sym(curve)
    au = [a[i][0] * u[0] + a[i][1] * u[1] + a[i][2] * u[2] for i in range(3)]
    bu = [b[i][0] * u[0] + b[i][1] * u[1] + b[i][2] * u[2] for i in range(3)]
    uau = u[0] * au[0] + u[1] * au[1] + u[2] * au[2]
    ubu = u[0] * bu[0] + u[1] * bu[1] + u[2] * bu[2]
    uw = u[0] * w[0] + u[1] * w[1] + u[2] * w[2]
    half = lambda m, k: (0.5 if k < 3 else 1.0) * m[k]
    expo = feature_coefs(
        LOG2E * (log_pre - 0.5 * uau),
        [LOG2E * v for v in au],
        [-LOG2E * half(inverse, k) for k in range(6)],
    )
    poly = feature_coefs(
        0.5 * (shift - uw + 0.5 * ubu),
        [0.5 * (w[i] - bu[i]) for i in range(3)],
        [0.5 * half(curve, k) for k in range(6)],
    )
    coef[...] = jnp.zeros(coef.shape, BF16)
    for p, entries in enumerate((expo, poly)):
        turn[...] = jnp.zeros(turn.shape, F32)
        for k, entry in enumerate(entries):
            turn[pl.ds(k * spots, spots), :] = entry
        for s in range(spots):
            lanes = pl.ds((p * spots + s) * LANES, LANES)
            for j, piece in enumerate(pieces(turn[pl.ds(s, FEATS, stride=spots), :])):
                coef[pl.ds(j * FEATS, FEATS), lanes] = piece
    root3 = 3.0 * GAUSS
    for start in range(0, count, CHUNK):
        size = min(CHUNK, count - start)
        power[...] = dot(tab[pl.ds(start, CHUNK), :], coef[...])

        def block(local):
            first = (start + local) * comps
            stores = []
            for row in range(rows):
                gd = []
                for q in range(4):
                    lane = (q * rows + row) * LANES
                    expo = power[pl.ds(local, SUB), lane : lane + LANES]
                    factor = power[pl.ds(local, SUB), spots * LANES + lane : spots * LANES + lane + LANES]
                    gd.append(jnp.exp2(expo) * factor)
                back, front = gd[0] + gd[1], gd[2] + gd[3]
                collided = (back + front, root3 * (front - back), root3 * ((gd[1] - gd[0]) + (gd[3] - gd[2])))
                for comp, value in enumerate(collided):
                    where = pl.ds(first + comp * rows + row, SUB, stride=comps)
                    stores.append((out, (where, slice(None)), adv[where, :] - value))
            return stores

        for_blocks(size, block, U_COLL)


def face_kernel(count, rows, col, tab, yrecv, out_hbm, out_v, wide, sems):
    comps = 3 * rows
    away = towards()
    scale = away.astype(F32)
    face = jnp.where(away == 1, rows - 1, 0)
    wide[...] = dot(tab[...], spread_table([(15, UNIT), (14, scale)], 1))
    low = iota((SUB, LANES), 0) % 4 < 2
    copies = []
    for j, start in enumerate(range(0, count, CHUNK)):
        size = min(CHUNK, count - start)
        part = pl.ds(start * comps, size * comps)
        out_v[part, :] = col[part, :]

        def block(local):
            at = start + local
            data = yrecv[pl.ds(at, SUB), :]
            turned = swap_pairs(data, low)
            speed = wide[pl.ds(at, SUB), 0:LANES]
            sign = wide[pl.ds(at, SUB), LANES : 2 * LANES]
            speed = jnp.where(sign < 0.0, speed, 0.0)
            value = speed * jnp.where(low, data, turned)
            slope = speed * jnp.where(low, turned, data)
            stores = []
            for comp, term in enumerate((value, slope, (3.0 * scale) * value)):
                where = pl.ds(at * comps + comp * rows + face, SUB, stride=comps)
                stores.append((out_v, (where, slice(None)), col[where, :] - term))
            return stores

        for_blocks(size, block, U_FACE)
        copies.append(pltpu.make_async_copy(out_v.at[part], out_hbm.at[part], sems.at[j]))
        copies[-1].start()
    for copy in copies:
        copy.wait()


def call(kernel, out_shape, scratch, ins, outs, name):
    return pl.pallas_call(
        kernel,
        out_shape=out_shape,
        in_specs=[pl.BlockSpec(memory_space=m) for m in ins],
        out_specs=jax.tree.map(lambda m: pl.BlockSpec(memory_space=m), outs),
        scratch_shapes=scratch,
        compiler_params=pltpu.CompilerParams(vmem_limit_bytes=VMEM_LIMIT),
        name=name,
    )


def exchange(value, axis, by):
    devices = lax.axis_size(axis)
    return lax.ppermute(value, axis, [(i, (i + by) % devices) for i in range(devices)])


def sum_over(value, axis, beside):
    devices = lax.axis_size(axis)
    step = 1
    while step < devices:
        if step == 4:
            value, *beside = lax.optimization_barrier((value, *beside))
        value = value + lax.ppermute(value, axis, [(i, i ^ step) for i in range(devices)])
        step *= 2
    return value, beside


def shards(state, tangent, orient, walls):
    count, _, rows, cols = state.shape
    comps = 3 * rows
    total_rows = count * comps
    padded = roundup(count, CHUNK)
    chunks = padded // CHUNK
    st = state.reshape(total_rows, cols)
    tn = tangent.reshape(total_rows, cols)
    signs = orient.T
    hold = [pltpu.with_memory_space_constraint(v, pltpu.HBM) for v in (signs, tn, st)]
    vm, hbm = pltpu.VMEM, pltpu.HBM
    shape = jax.ShapeDtypeStruct
    ysend, xsend, mom, tab, tan_v = call(
        functools.partial(pre_kernel, count, rows),
        (
            shape((count, cols), F32),
            shape((SUB, padded), F32),
            shape((2 * comps * 10, cols), F32),
            shape((padded, LANES), BF16),
            shape((padded * comps, cols), F32),
        ),
        [
            pltpu.VMEM((2, count), jnp.int32),
            pltpu.VMEM((FEATS, padded), F32),
            pltpu.VMEM((padded, 2 * LANES), F32),
            pltpu.VMEM((padded, LANES), F32),
            pltpu.VMEM((padded * comps, cols), F32),
            pltpu.SemaphoreType.DMA((2 * chunks + 1,)),
        ],
        (hbm, hbm, hbm),
        (vm, vm, vm, vm, vm),
        "pack_and_moments",
    )(*hold)
    yrecv = lax.ppermute(ysend, "gy", [(0, 1), (1, 0)])
    single = lax.axis_size("gx") == 2
    edges = (exchange(xsend, "gx", 1),) + (() if single else (exchange(xsend, "gx", -1),))
    mom, edges = sum_over(mom, "vert", edges)
    edges += [] if single else [signs]
    adv = call(
        functools.partial(transport_kernel, count, rows, cols, single),
        shape((total_rows, cols), F32),
        [pltpu.VMEM((padded, (5 + 2 * rows) * LANES), F32)],
        (vm,) * (3 + len(edges)),
        vm,
        "transport",
    )(tan_v, tab, walls, *edges)
    col = call(
        functools.partial(collide_kernel, count, rows),
        shape((total_rows, cols), F32),
        [
            pltpu.VMEM((4 * rows * 24, LANES), F32),
            pltpu.VMEM((FEATS * 4 * rows, LANES), F32),
            pltpu.VMEM((LANES, 8 * rows * LANES), BF16),
            pltpu.VMEM((CHUNK, 8 * rows * LANES), F32),
        ],
        (vm, vm, vm),
        vm,
        "collide",
    )(mom, tab, adv)
    out = call(
        functools.partial(face_kernel, count, rows),
        shape((total_rows, cols), F32),
        [
            pltpu.VMEM((total_rows, cols), F32),
            pltpu.VMEM((padded, 2 * LANES), F32),
            pltpu.SemaphoreType.DMA((chunks,)),
        ],
        (vm, vm, vm),
        hbm,
        "faces",
    )(col, tab, yrecv)
    return out.reshape(state.shape)


def solution(mesh):
    placed = (
        P("vert", None, "gy", "gx"),
        P("vert", None, "gy", "gx"),
        P("vert", None),
        P(None, "gx"),
    )
    return jax.shard_map(
        shards, mesh=mesh, in_specs=placed, out_specs=P("vert", None, "gy", "gx"), check_vma=False
    )
```

```python
import functools
import math

import jax
import jax.numpy as jnp
from jax import lax
from jax.experimental import pallas as pl
from jax.experimental.pallas import tpu as pltpu
from jax.sharding import PartitionSpec as P

NVX = 20
GAUSS = 0.5773502691896258
XI_SIGNS = (-1.0, -1.0, 1.0, 1.0)
ETA_SIGNS = (-1.0, 1.0, -1.0, 1.0)
DUOS = ((0, 0), (1, 1), (2, 2), (0, 1), (0, 2), (1, 2))
LOG_TWO_PI = math.log(2.0 * math.pi)
LOG2E = 1.0 / math.log(2.0)
HALF = NVX // 2
SPACING = 5.0 / HALF
UNIT = 0.5 * SPACING
FEATS = 16
SUB = 8
IN_FLIGHT = 64
WORK = 4500 * 10**6
LANES = 128
CHUNK = 256
CHUNK_OUT = 128
U_PACK, U_TRANS, U_COLL, U_FACE = 32, 32, 16, 16
F32 = jnp.float32
BF16 = jnp.bfloat16
VMEM_LIMIT = 16 * 1024 * 1024


def roundup(value, unit):
    return -(-value // unit) * unit


def for_blocks(count, body, unroll):
    whole = count // SUB
    rounds = whole // unroll

    def group(firsts):
        for ref, where, value in [store for first in firsts for store in body(first)]:
            ref[where] = value

    def step(i, carry):
        group([pl.multiple_of((i * unroll + k) * SUB, SUB) for k in range(unroll)])
        return carry

    if rounds == 1:
        group([k * SUB for k in range(unroll)])
    elif rounds:
        lax.fori_loop(0, rounds, step, 0)
    left = [k * SUB for k in range(rounds * unroll, whole)]
    if left:
        group(left)
    if count % SUB:
        group([count - SUB])


def swap_pairs(value, low):
    return jnp.where(low, pltpu.roll(value, SUB - 2, 0), pltpu.roll(value, 2, 0))


def iota(shape, dim):
    return lax.broadcasted_iota(jnp.int32, shape, dim)


def towards():
    return jnp.where(lax.axis_index("gy") == 0, 1, -1)


def fill_features(feat, orient_ref, count):
    feat[...] = jnp.zeros(feat.shape, F32)
    slot = (iota((1, count), 1) + lax.axis_index("vert") * count).astype(F32)
    jz = jnp.floor((slot + 0.5) * (1.0 / (4 * HALF * HALF)))
    slot = slot - jz * (4.0 * HALF * HALF)
    mx = jnp.floor((slot + 0.5) * (1.0 / (4 * HALF)))
    slot = slot - mx * (4.0 * HALF)
    my = jnp.floor((slot + 0.5) * 0.25)
    sx = (2 * orient_ref[0:1, :] - 1).astype(F32)
    sy = (2 * orient_ref[1:2, :] - 1).astype(F32)
    ox = sx * (2.0 * mx + 1.0)
    oy = sy * (2.0 * my + 1.0)
    oz = 2.0 * jz - (2.0 * HALF - 1.0)
    cross = (ox * oy, ox * oz, oy * oz)
    high = [jnp.floor(c * 0.0625) * 16.0 for c in cross]
    low = [c - h for c, h in zip(cross, high)]
    rows = [jnp.ones_like(ox), ox, oy, oz, mx * (mx + 1.0), my * (my + 1.0), 0.25 * (oz * oz - 1.0)]
    rows = rows + high + low + [sx, sy, 2.0 * my + 1.0]
    for k, row in enumerate(rows):
        feat[k : k + 1, 0:count] = row


def spread_table(columns, step):
    rows = iota((LANES, LANES * len(columns)), 0)
    blocks = iota((LANES, LANES * len(columns)), 1) // LANES
    out = jnp.zeros(rows.shape, F32)
    for j, (row, scale) in enumerate(columns):
        out = jnp.where((rows == row) & (blocks == j), scale, out)
    return out.astype(BF16)


def pieces(value):
    high = value.astype(BF16)
    rest = value - high.astype(F32)
    mid = rest.astype(BF16)
    low = (rest - mid.astype(F32)).astype(BF16)
    return high, mid, low


def dot(left, right):
    return jnp.dot(left, right, preferred_element_type=F32)


def pre_kernel(count, rows, orient_hbm, tan_hbm, st_hbm, ysend, xsend, mom, tab, tan_v, orient_ref, total_v, feat, wide, edge, st_v, sems):
    comps = 3 * rows
    padded = feat.shape[1]
    starts = list(range(0, padded, CHUNK))
    copies = []
    for a, (src, dst) in enumerate(((tan_hbm, tan_v), (st_hbm, st_v))):
        for j, start in enumerate(starts):
            size = min(CHUNK, count - start) * comps
            part = pl.ds(start * comps, size)
            copies.append(pltpu.make_async_copy(src.at[part], dst.at[part], sems.at[a * len(starts) + j]))
    signs = pltpu.make_async_copy(orient_hbm, orient_ref, sems.at[2 * len(starts)])
    signs.start()
    for copy in copies[:IN_FLIGHT]:
        copy.start()
    tail = (padded - count) * comps
    for buf in (tan_v, st_v):
        if tail:
            buf[pl.ds(count * comps, tail), :] = jnp.zeros((tail, LANES), F32)
    edge[...] = jnp.zeros(edge.shape, F32)
    signs.wait()
    fill_features(feat, orient_ref, count)
    table = feat[...]
    spare = jnp.zeros((LANES - 3 * FEATS, padded), F32)
    flipped = jnp.concatenate([table, table, table, spare], axis=0).T.astype(BF16)
    tab[...] = flipped
    away = towards()
    scale = away.astype(F32)
    wide[...] = dot(flipped, spread_table([(13, 1.0), (14, 1.0)], 1))
    face = jnp.where(away == 1, rows - 1, 0)
    low = iota((SUB, LANES), 0) % 4 < 2
    lane = iota((SUB, LANES), 1)
    table = table.astype(BF16)
    sums = [[total_v.at[pl.ds((a * comps + c) * FEATS, FEATS)] for c in range(comps)] for a in range(2)]
    for a, buf in enumerate((tan_v, st_v)):
        for j, start in enumerate(starts):
            copies[a * len(starts) + j].wait()
            for copy in copies[a * len(starts) + j + IN_FLIGHT :][:1]:
                copy.start()

            def pack(local):
                first = start + local
                at = lambda comp, row: buf[pl.ds(first * comps + comp * rows + row, SUB, stride=comps), :]
                where = (pl.ds(first, SUB), slice(None))
                sx = wide[pl.ds(first, SUB), 0:LANES]
                sy = wide[pl.ds(first, SUB), LANES : 2 * LANES]
                center, grad_x, grad_y = at(0, face), at(1, face), at(2, face)
                out_y = center + sy * grad_y
                own = jnp.where(low, out_y, grad_x)
                other = jnp.where(low, grad_x, out_y)
                packed = jnp.where(sy * scale > 0.0, own, swap_pairs(other, low))
                right = sx > 0.0
                acc = jnp.zeros((SUB, LANES), F32)
                for row in range(rows):
                    slope = at(2, row)
                    value = at(0, row) + sx * at(1, row)
                    for j, piece in ((2 * row, value), (2 * row + 1, slope)):
                        here = jnp.where(right, pltpu.roll(piece, 1 + j, 1), pltpu.roll(piece, j, 1) if j else piece)
                        acc = jnp.where(lane == j, here, acc)
                return [(ysend, where, packed), (edge, where, acc)]

            if a == 0:
                for_blocks(min(CHUNK, count - start), pack, U_PACK)
            size = min(CHUNK, padded - start)
            part = table[:, start : start + size]
            for c in range(comps):
                data = buf[pl.ds(start * comps + c, size, stride=comps), :]
                high = data.astype(BF16)
                rest = (data - high.astype(F32)).astype(BF16)
                new = dot(part, high) + dot(part, rest)
                sums[a][c][...] = new if j == 0 else sums[a][c][...] + new
        if a == 0:
            xsend[...] = edge[...].T[0 : xsend.shape[0], :]
        for c in range(comps):
            total = sums[a][c][...]
            squares = 4.0 * total[4:7] + total[0:1]
            cross = total[7:10] + total[10:13]
            slot = (1 - a) * comps + c
            mom[pl.ds(slot * 8, 4), :] = total[0:4]
            mom[pl.ds(slot * 8 + 4, 3), :] = squares
            mom[pl.ds(slot * 8 + 7, 1), :] = cross[0:1]
            mom[pl.ds(2 * comps * 8 + slot * 2, 2), :] = cross[1:3]


def transport_kernel(count, rows, cols, single, *refs):
    tan_v, tab, walls, behind = refs[:4]
    adv, wide = refs[-2:]
    comps = 3 * rows
    padded = tab.shape[0]
    away = towards()
    scale = away.astype(F32)
    arrived = behind[...]
    if not single:
        ahead, signs = refs[4:6]
        spare = [jnp.zeros((1, padded - count), jnp.int32)] if padded > count else []
        right_row = jnp.concatenate([signs[0:1, :]] + spare, axis=1) == 1
        arrived = jnp.where(right_row, arrived, ahead[...])
    spare = jnp.zeros((LANES - 3 * SUB, padded), F32)
    parts = [piece.astype(F32) for piece in pieces(arrived)]
    edges = jnp.concatenate(parts + [spare], axis=0).T.astype(BF16)
    cols_w = [(1, UNIT), (2, UNIT), (15, UNIT), (13, 1.0), (14, scale)]
    wide[:, 0 : 5 * LANES] = dot(tab[...], spread_table(cols_w, 1))
    r = iota((LANES, LANES * 2 * rows), 0)
    b = iota((LANES, LANES * 2 * rows), 1) // LANES
    pick = jnp.where((r % SUB == b) & (r < 3 * SUB), 1.0, 0.0).astype(BF16)
    wide[:, 5 * LANES : (5 + 2 * rows) * LANES] = dot(edges, pick)
    sub = iota((SUB, LANES), 0)
    low = sub % 4 < 2
    lane = iota((SUB, LANES), 1)
    ends = jnp.where(lane == cols - 1, 1.0, 0.0) - jnp.where(lane == 0, 1.0, 0.0)
    wall_row = jnp.where(away == 1, walls[0:1, :], walls[1:2, :]).astype(F32)
    wall = jnp.broadcast_to(wall_row, (SUB, LANES))
    order = [jnp.where(away == 1, k, rows - 1 - k) for k in range(rows)]

    def block(start):
        at = lambda comp, row: tan_v[pl.ds(start * comps + comp * rows + row, SUB, stride=comps), :]
        col = lambda j: wide[pl.ds(start, SUB), j * LANES : (j + 1) * LANES]
        vx, vy, ay, sx, toward_sign = (col(j) for j in range(5))
        ax = vx * sx
        sy = toward_sign * scale
        right = sx > 0.0
        toward = toward_sign > 0.0
        outgoing = sx * ends > 0.0
        center = [at(0, order[k]) for k in range(rows)]
        grad_x = [at(1, order[k]) for k in range(rows)]
        grad_y = [at(2, order[k]) for k in range(rows)]
        out_y = [c + sy * g for c, g in zip(center, grad_y)]
        stores = []
        for k in range(rows):
            ecol = lambda j: wide[pl.ds(start, SUB), pl.ds(pl.multiple_of((5 + 2 * order[k] + j) * LANES, LANES), LANES)]
            out_x = center[k] + sx * grad_x[k]

            def inflow(piece, received):
                mixed = jnp.where(outgoing, received, piece)
                return jnp.where(right, pltpu.roll(mixed, 1, 1), pltpu.roll(mixed, cols - 1, 1))

            in_x = inflow(out_x, ecol(0))
            in_xs = inflow(grad_y[k], ecol(1))
            if k == 0:
                near_v = wall * swap_pairs(out_y[0], low)
                near_s = wall * swap_pairs(grad_x[0], low)
            else:
                near_v, near_s = out_y[k - 1], grad_x[k - 1]
            if k == rows - 1:
                far_v, far_s = jnp.zeros_like(near_v), jnp.zeros_like(near_s)
            else:
                far_v, far_s = out_y[k + 1], grad_x[k + 1]
            in_y = jnp.where(toward, near_v, far_v)
            in_ys = jnp.where(toward, near_s, far_s)
            twice = 2.0 * center[k]
            mean = ax * (out_x - in_x) + ay * (out_y[k] - in_y) + twice
            rate_x = 3.0 * vx * (out_x + in_x - twice) + ay * (grad_x[k] - in_ys) + 2.0 * grad_x[k]
            rate_y = ax * (grad_y[k] - in_xs) + 3.0 * vy * (out_y[k] + in_y - twice) + 2.0 * grad_y[k]
            for comp, value in enumerate((mean, rate_x, rate_y)):
                where = pl.ds(start * comps + comp * rows + order[k], SUB, stride=comps)
                stores.append((adv, (where, slice(None)), value))
        return stores

    for_blocks(count, block, U_TRANS)


def sym(entries):
    grid = [[None] * 3 for _ in range(3)]
    for k, (i, j) in enumerate(DUOS):
        grid[i][j] = entries[k]
        grid[j][i] = entries[k]
    return grid


def point_params(moments):
    density = moments[0]
    inv_density = 1.0 / density
    u = [moments[1 + i] * inv_density for i in range(3)]
    second = [moments[4 + k] for k in range(6)]
    theta = [second[k] * inv_density - u[i] * u[j] for k, (i, j) in enumerate(DUOS)]
    temp = (theta[0] + theta[1] + theta[2]) / 3.0
    tensor = [(1.5 * temp if i == j else 0.0) - 0.5 * theta[k] for k, (i, j) in enumerate(DUOS)]
    t = sym(tensor)
    cof = [
        t[1][1] * t[2][2] - t[1][2] * t[1][2],
        t[0][0] * t[2][2] - t[0][2] * t[0][2],
        t[0][0] * t[1][1] - t[0][1] * t[0][1],
        t[0][2] * t[1][2] - t[0][1] * t[2][2],
        t[0][1] * t[1][2] - t[0][2] * t[1][1],
        t[0][1] * t[0][2] - t[0][0] * t[1][2],
    ]
    det = t[0][0] * cof[0] + t[0][1] * cof[3] + t[0][2] * cof[4]
    inv_det = 1.0 / det
    inverse = [entry * inv_det for entry in cof]
    log_pre = jnp.log(density) - 1.5 * LOG_TWO_PI - 0.5 * jnp.log(det)
    drho = moments[10]
    du = [(moments[11 + i] - u[i] * drho) * inv_density for i in range(3)]
    ratio = drho * inv_density
    dtheta = [
        moments[14 + k] * inv_density - second[k] * inv_density * ratio - (du[i] * u[j] + u[i] * du[j])
        for k, (i, j) in enumerate(DUOS)
    ]
    dtemp = (dtheta[0] + dtheta[1] + dtheta[2]) / 3.0
    dtensor = [(1.5 * dtemp if i == j else 0.0) - 0.5 * dtheta[k] for k, (i, j) in enumerate(DUOS)]
    a, d = sym(inverse), sym(dtensor)
    trace = sum(a[i][j] * d[j][i] for i in range(3) for j in range(3))
    shift = ratio - 0.5 * trace
    w = [a[i][0] * du[0] + a[i][1] * du[1] + a[i][2] * du[2] for i in range(3)]
    ad = [[a[i][0] * d[0][j] + a[i][1] * d[1][j] + a[i][2] * d[2][j] for j in range(3)] for i in range(3)]
    curve = [ad[i][0] * a[0][j] + ad[i][1] * a[1][j] + ad[i][2] * a[2][j] for i, j in DUOS]
    return u, inverse, log_pre, shift, w, curve


def feature_coefs(const, linear, quad):
    square = [UNIT * UNIT * quad[k] for k in range(6)]
    const = const + square[0] + square[1] + square[2]
    return [const] + [UNIT * l for l in linear] + [4.0 * s for s in square[:3]] + square[3:] + square[3:]


def collide_kernel(count, rows, mom, tab, adv, out_hbm, kept, raw, turn, coef, power, out, sems):
    comps = 3 * rows
    spots = 4 * rows
    weight = SPACING**3
    scales = [weight] + [weight * UNIT] * 3 + [weight * UNIT * UNIT] * 4
    row_scale = jnp.zeros((SUB, LANES), F32)
    sub = iota((SUB, LANES), 0)
    for k, s in enumerate(scales):
        row_scale = jnp.where(sub == k, s, row_scale)
    for a in range(2):
        for row in range(rows):
            first = [row_scale * mom[pl.ds((a * comps + c * rows + row) * 8, 8), :] for c in range(3)]
            last = [
                (weight * UNIT * UNIT) * mom[pl.ds(2 * comps * 8 + (a * comps + c * rows + row) * 2, 2), :]
                for c in range(3)
            ]
            for q in range(4):
                mix = lambda v: v[0] + (XI_SIGNS[q] * GAUSS) * v[1] + (ETA_SIGNS[q] * GAUSS) * v[2]
                base = (q * rows + row) * 24 + a * 10
                raw[pl.ds(base, 8), :] = mix(first)
                raw[pl.ds(base + 8, 2), :] = mix(last)
    moments = [raw[pl.ds(k, spots, stride=24), :] for k in range(20)]
    u, inverse, log_pre, shift, w, curve = point_params(moments)
    a, b = sym(inverse), sym(curve)
    au = [a[i][0] * u[0] + a[i][1] * u[1] + a[i][2] * u[2] for i in range(3)]
    bu = [b[i][0] * u[0] + b[i][1] * u[1] + b[i][2] * u[2] for i in range(3)]
    uau = u[0] * au[0] + u[1] * au[1] + u[2] * au[2]
    ubu = u[0] * bu[0] + u[1] * bu[1] + u[2] * bu[2]
    uw = u[0] * w[0] + u[1] * w[1] + u[2] * w[2]
    half = lambda m, k: (0.5 if k < 3 else 1.0) * m[k]
    expo = feature_coefs(
        LOG2E * (log_pre - 0.5 * uau),
        [LOG2E * v for v in au],
        [-LOG2E * half(inverse, k) for k in range(6)],
    )
    poly = feature_coefs(
        0.5 * (shift - uw + 0.5 * ubu),
        [0.5 * (w[i] - bu[i]) for i in range(3)],
        [0.5 * half(curve, k) for k in range(6)],
    )
    coef[...] = jnp.zeros(coef.shape, BF16)
    for p, entries in enumerate((expo, poly)):
        turn[...] = jnp.zeros(turn.shape, F32)
        for k, entry in enumerate(entries):
            turn[pl.ds(k * spots, spots), :] = entry
        for s in range(spots):
            lanes = pl.ds((p * spots + s) * LANES, LANES)
            for j, piece in enumerate(pieces(turn[pl.ds(s, FEATS, stride=spots), :])):
                coef[pl.ds(j * FEATS, FEATS), lanes] = piece
    root3 = 3.0 * GAUSS
    face = jnp.where(towards() == 1, rows - 1, 0)
    copies = []
    for j, start in enumerate(range(0, count, CHUNK_OUT)):
        size = min(CHUNK_OUT, count - start)
        half_power = power.at[j % 2]
        half_power[...] = dot(tab[pl.ds(start, CHUNK_OUT), :], coef[...])

        def block(local):
            first = (start + local) * comps
            stores = []
            for row in range(rows):
                gd = []
                for q in range(4):
                    lane = (q * rows + row) * LANES
                    expo = half_power[pl.ds(local, SUB), lane : lane + LANES]
                    factor = half_power[pl.ds(local, SUB), spots * LANES + lane : spots * LANES + lane + LANES]
                    gd.append(jnp.exp2(expo) * factor)
                back, front = gd[0] + gd[1], gd[2] + gd[3]
                collided = (back + front, root3 * (front - back), root3 * ((gd[1] - gd[0]) + (gd[3] - gd[2])))
                for comp, value in enumerate(collided):
                    where = pl.ds(first + comp * rows + row, SUB, stride=comps)
                    stores.append((out, (where, slice(None)), adv[where, :] - value))
            return stores

        for_blocks(size, block, U_COLL)
        part = pl.ds(start * comps, size * comps)
        copies.append(pltpu.make_async_copy(out.at[part], out_hbm.at[part], sems.at[j]))
        copies[-1].start()
        part = pl.ds(start * 3, size * 3)
        kept[part, :] = out[pl.ds(start * comps + face, size * 3, stride=rows), :]
    for copy in copies:
        copy.wait()


def face_kernel(count, rows, kept, tab, yrecv, before, out, face_v, wide, sems):
    scale = towards().astype(F32)
    face = jnp.where(towards() == 1, rows - 1, 0)
    wide[...] = dot(tab[...], spread_table([(15, UNIT), (14, scale)], 1))
    low = iota((SUB, LANES), 0) % 4 < 2
    copies = []
    for j, start in enumerate(range(0, count, CHUNK_OUT)):
        size = min(CHUNK_OUT, count - start)

        def block(local):
            at = start + local
            data = yrecv[pl.ds(at, SUB), :]
            turned = swap_pairs(data, low)
            speed = wide[pl.ds(at, SUB), 0:LANES]
            sign = wide[pl.ds(at, SUB), LANES : 2 * LANES]
            speed = jnp.where(sign < 0.0, speed, 0.0)
            value = speed * jnp.where(low, data, turned)
            slope = speed * jnp.where(low, turned, data)
            stores = []
            for comp, term in enumerate((value, slope, (3.0 * scale) * value)):
                where = pl.ds(at * 3 + comp, SUB, stride=3)
                stores.append((face_v, (where, slice(None)), kept[where, :] - term))
            return stores

        for_blocks(size, block, U_FACE)
        part = pl.ds(start * 3, size * 3)
        copies.append(pltpu.make_async_copy(face_v.at[part], out.at[part, face], sems.at[j]))
        copies[-1].start()
    for copy in copies:
        copy.wait()


def call(kernel, out_shape, scratch, ins, outs, name, aliases={}, work=0):
    return pl.pallas_call(
        kernel,
        out_shape=out_shape,
        in_specs=[pl.BlockSpec(memory_space=m) for m in ins],
        out_specs=jax.tree.map(lambda m: pl.BlockSpec(memory_space=m), outs),
        scratch_shapes=scratch,
        compiler_params=pltpu.CompilerParams(vmem_limit_bytes=VMEM_LIMIT),
        input_output_aliases=aliases,
        cost_estimate=pl.CostEstimate(flops=work, transcendentals=0, bytes_accessed=0) if work else None,
        name=name,
    )


def exchange(value, axis, by):
    devices = lax.axis_size(axis)
    return lax.ppermute(value, axis, [(i, (i + by) % devices) for i in range(devices)])


def sum_over(value, axis):
    devices = lax.axis_size(axis)
    step = 1
    while step < devices:
        value = value + lax.ppermute(value, axis, [(i, i ^ step) for i in range(devices)])
        step *= 2
    return value


def shards(state, tangent, orient, walls):
    count, _, rows, cols = state.shape
    comps = 3 * rows
    total_rows = count * comps
    padded = roundup(count, CHUNK)
    chunks = padded // CHUNK
    st = state.reshape(total_rows, cols)
    tn = tangent.reshape(total_rows, cols)
    signs = orient.T
    hold = [pltpu.with_memory_space_constraint(v, pltpu.HBM) for v in (signs, tn, st)]
    vm, hbm = pltpu.VMEM, pltpu.HBM
    shape = jax.ShapeDtypeStruct
    ysend, xsend, mom, tab, tan_v = call(
        functools.partial(pre_kernel, count, rows),
        (
            shape((count, cols), F32),
            shape((SUB, padded), F32),
            shape((2 * comps * 10, cols), F32),
            shape((padded, LANES), BF16),
            shape((padded * comps, cols), F32),
        ),
        [
            pltpu.VMEM((2, count), jnp.int32),
            pltpu.VMEM((2 * comps * FEATS, cols), F32),
            pltpu.VMEM((FEATS, padded), F32),
            pltpu.VMEM((padded, 2 * LANES), F32),
            pltpu.VMEM((padded, LANES), F32),
            pltpu.VMEM((padded * comps, cols), F32),
            pltpu.SemaphoreType.DMA((2 * chunks + 1,)),
        ],
        (hbm, hbm, hbm),
        (vm, vm, vm, vm, vm),
        "pack_and_moments",
    )(*hold)
    yrecv = lax.ppermute(ysend, "gy", [(0, 1), (1, 0)])
    single = lax.axis_size("gx") == 2
    edges = (exchange(xsend, "gx", 1),) + (() if single else (exchange(xsend, "gx", -1),))
    mom = sum_over(mom, "vert")
    edges += () if single else (signs,)
    adv = call(
        functools.partial(transport_kernel, count, rows, cols, single),
        shape((total_rows, cols), F32),
        [pltpu.VMEM((padded, (5 + 2 * rows) * LANES), F32)],
        (vm,) * (3 + len(edges)),
        vm,
        "transport",
        work=WORK,
    )(tan_v, tab, walls, *edges)
    col, kept = call(
        functools.partial(collide_kernel, count, rows),
        (shape((total_rows, cols), F32), shape((count * 3, cols), F32)),
        [
            pltpu.VMEM((4 * rows * 24, LANES), F32),
            pltpu.VMEM((FEATS * 4 * rows, LANES), F32),
            pltpu.VMEM((LANES, 8 * rows * LANES), BF16),
            pltpu.VMEM((2, CHUNK_OUT, 8 * rows * LANES), F32),
            pltpu.VMEM((total_rows, cols), F32),
            pltpu.SemaphoreType.DMA((padded // CHUNK_OUT,)),
        ],
        (vm, vm, vm),
        (hbm, vm),
        "collide",
    )(mom, tab, adv)
    out = call(
        functools.partial(face_kernel, count, rows),
        shape((count * 3, rows, cols), F32),
        [
            pltpu.VMEM((count * 3, cols), F32),
            pltpu.VMEM((padded, 2 * LANES), F32),
            pltpu.SemaphoreType.DMA((padded // CHUNK_OUT,)),
        ],
        (vm, vm, vm, hbm),
        hbm,
        "faces",
        {3: 0},
    )(kept, tab, yrecv, col.reshape(count * 3, rows, cols))
    return out.reshape(state.shape)


def solution(mesh):
    placed = (
        P("vert", None, "gy", "gx"),
        P("vert", None, "gy", "gx"),
        P("vert", None),
        P(None, "gx"),
    )
    return jax.shard_map(
        shards, mesh=mesh, in_specs=placed, out_specs=P("vert", None, "gy", "gx"), check_vma=False
    )
```

```python
import functools
import math

import jax
import jax.numpy as jnp
from jax import lax
from jax.experimental import pallas as pl
from jax.experimental.pallas import tpu as pltpu
from jax.sharding import PartitionSpec as P

NVX = 20
GAUSS = 0.5773502691896258
XI_SIGNS = (-1.0, -1.0, 1.0, 1.0)
ETA_SIGNS = (-1.0, 1.0, -1.0, 1.0)
DUOS = ((0, 0), (1, 1), (2, 2), (0, 1), (0, 2), (1, 2))
LOG_TWO_PI = math.log(2.0 * math.pi)
LOG2E = 1.0 / math.log(2.0)
HALF = NVX // 2
SPACING = 5.0 / HALF
UNIT = 0.5 * SPACING
FEATS = 16
SUB = 8
IN_FLIGHT = 64
WORK = 4500 * 10**6
LANES = 128
CHUNK = 256
CHUNK_OUT = 128
U_PACK, U_EDGE, U_TRANS, U_COLL, U_FACE = 32, 31, 16, 16, 16
F32 = jnp.float32
BF16 = jnp.bfloat16
VMEM_LIMIT = 16 * 1024 * 1024


def roundup(value, unit):
    return -(-value // unit) * unit


def for_blocks(count, body, unroll):
    whole = count // SUB
    rounds = whole // unroll

    def group(firsts):
        for ref, where, value in [store for first in firsts for store in body(first)]:
            ref[where] = value

    def step(i, carry):
        group([pl.multiple_of((i * unroll + k) * SUB, SUB) for k in range(unroll)])
        return carry

    if rounds == 1:
        group([k * SUB for k in range(unroll)])
    elif rounds:
        lax.fori_loop(0, rounds, step, 0)
    left = [k * SUB for k in range(rounds * unroll, whole)]
    if left:
        group(left)
    if count % SUB:
        group([count - SUB])


def swap_rows(value, first, by):
    return jnp.where(first, pltpu.roll(value, SUB - by, 0), pltpu.roll(value, by, 0))


def iota(shape, dim):
    return lax.broadcasted_iota(jnp.int32, shape, dim)


def towards():
    return jnp.where(lax.axis_index("gy") == 0, 1, -1)


def fill_features(feat, orient_ref, count):
    feat[...] = jnp.zeros(feat.shape, F32)
    slot = (iota((1, count), 1) + lax.axis_index("vert") * count).astype(F32)
    jz = jnp.floor((slot + 0.5) * (1.0 / (4 * HALF * HALF)))
    slot = slot - jz * (4.0 * HALF * HALF)
    mx = jnp.floor((slot + 0.5) * (1.0 / (4 * HALF)))
    slot = slot - mx * (4.0 * HALF)
    my = jnp.floor((slot + 0.5) * 0.25)
    sx = (2 * orient_ref[0:1, :] - 1).astype(F32)
    sy = (2 * orient_ref[1:2, :] - 1).astype(F32)
    ox = sx * (2.0 * mx + 1.0)
    oy = sy * (2.0 * my + 1.0)
    oz = 2.0 * jz - (2.0 * HALF - 1.0)
    cross = (ox * oy, ox * oz, oy * oz)
    high = [jnp.floor(c * 0.0625) * 16.0 for c in cross]
    low = [c - h for c, h in zip(cross, high)]
    rows = [jnp.ones_like(ox), ox, oy, oz, mx * (mx + 1.0), my * (my + 1.0), 0.25 * (oz * oz - 1.0)]
    rows = rows + high + low + [sx, sy, 2.0 * my + 1.0]
    for k, row in enumerate(rows):
        feat[k : k + 1, 0:count] = row


def spread_table(columns):
    rows = iota((LANES, LANES * len(columns)), 0)
    blocks = iota((LANES, LANES * len(columns)), 1) // LANES
    out = jnp.zeros(rows.shape, F32)
    for j, (row, scale) in enumerate(columns):
        out = jnp.where((rows == row) & (blocks == j), scale, out)
    return out.astype(BF16)


def pieces(value):
    high = value.astype(BF16)
    rest = value - high.astype(F32)
    mid = rest.astype(BF16)
    low = (rest - mid.astype(F32)).astype(BF16)
    return high, mid, low


def dot(left, right):
    return jnp.dot(left, right, preferred_element_type=F32)


def pre_kernel(count, rows, orient_hbm, tan_hbm, st_hbm, ysend, mom, tab, tan_v, wide, orient_ref, total_v, feat, st_v, sems):
    comps = 3 * rows
    padded = feat.shape[1]
    starts = list(range(0, padded, CHUNK))
    copies = []
    for a, (src, dst) in enumerate(((tan_hbm, tan_v), (st_hbm, st_v))):
        for j, start in enumerate(starts):
            size = min(CHUNK, count - start) * comps
            part = pl.ds(start * comps, size)
            copies.append(pltpu.make_async_copy(src.at[part], dst.at[part], sems.at[a * len(starts) + j]))
    signs = pltpu.make_async_copy(orient_hbm, orient_ref, sems.at[2 * len(starts)])
    signs.start()
    for copy in copies[:IN_FLIGHT]:
        copy.start()
    tail = (padded - count) * comps
    for buf in (tan_v, st_v):
        if tail:
            buf[pl.ds(count * comps, tail), :] = jnp.zeros((tail, LANES), F32)
    signs.wait()
    fill_features(feat, orient_ref, count)
    table = feat[...]
    spare = jnp.zeros((LANES - 3 * FEATS, padded), F32)
    flipped = jnp.concatenate([table, table, table, spare], axis=0).T.astype(BF16)
    tab[...] = flipped
    away = towards()
    scale = away.astype(F32)
    for j, column in enumerate(((1, UNIT), (15, UNIT), (13, 1.0), (14, scale))):
        wide[pl.ds(j * padded, padded), :] = dot(flipped, spread_table([column]))
    face = jnp.where(away == 1, rows - 1, 0)
    low = iota((SUB, LANES), 0) % 4 < 2
    table = table.astype(BF16)
    sums = [[total_v.at[pl.ds((a * comps + c) * FEATS, FEATS)] for c in range(comps)] for a in range(2)]
    for a, buf in enumerate((tan_v, st_v)):
        for j, start in enumerate(starts):
            copies[a * len(starts) + j].wait()
            for copy in copies[a * len(starts) + j + IN_FLIGHT :][:1]:
                copy.start()

            def pack(local):
                first = start + local
                at = lambda comp, row: buf[pl.ds(first * comps + comp * rows + row, SUB, stride=comps), :]
                toward = wide[pl.ds(3 * padded + first, SUB), :]
                center, grad_x, grad_y = at(0, face), at(1, face), at(2, face)
                out_y = center + (toward * scale) * grad_y
                own = jnp.where(low, out_y, grad_x)
                other = jnp.where(low, grad_x, out_y)
                packed = jnp.where(toward > 0.0, own, swap_rows(other, low, 2))
                return [(ysend, (pl.ds(first, SUB), slice(None)), packed)]

            if a == 0:
                for_blocks(min(CHUNK, count - start), pack, U_PACK)
            size = min(CHUNK, padded - start)
            part = table[:, start : start + size]
            for c in range(comps):
                data = buf[pl.ds(start * comps + c, size, stride=comps), :]
                high = data.astype(BF16)
                rest = (data - high.astype(F32)).astype(BF16)
                new = dot(part, high) + dot(part, rest)
                sums[a][c][...] = new if j == 0 else sums[a][c][...] + new
        for c in range(comps):
            total = sums[a][c][...]
            squares = 4.0 * total[4:7] + total[0:1]
            cross = total[7:10] + total[10:13]
            slot = (1 - a) * comps + c
            mom[pl.ds(slot * 8, 4), :] = total[0:4]
            mom[pl.ds(slot * 8 + 4, 3), :] = squares
            mom[pl.ds(slot * 8 + 7, 1), :] = cross[0:1]
            mom[pl.ds(2 * comps * 8 + slot * 2, 2), :] = cross[1:3]


def pair_reader(tan_v, comps, rows, start):
    return lambda comp, row, odd: tan_v[
        pl.ds((2 * start + odd) * comps + comp * rows + row, SUB, stride=2 * comps), :
    ]


def edge_kernel(count, rows, tan_v, wide, xsend, edge):
    comps = 3 * rows
    lane = iota((SUB, LANES), 1)
    last = lane == LANES - 1
    inside = jnp.logical_not(last | (lane == 0))
    sign = jnp.where(last, 1.0, -1.0)
    tail = edge.shape[0] - count // 2
    if tail:
        edge[pl.ds(count // 2, tail), :] = jnp.zeros((tail, LANES), F32)

    def block(start):
        at = pair_reader(tan_v, comps, rows, start)
        even = wide[pl.ds(4 * edge.shape[0] + 2 * start, SUB, stride=2), :] * sign > 0.0
        held = []
        for row in range(rows):
            center, grad_x, grad_y = (jnp.where(even, at(c, row, 0), at(c, row, 1)) for c in range(3))
            held.append(jnp.where(inside, 0.0, center + sign * grad_x))
            held.append(jnp.where(inside, 0.0, grad_y))
        shift = 2
        while len(held) > 1:
            pairs = zip(held[0::2], held[1::2])
            held = [p + pltpu.roll(q, shift, 1) for p, q in pairs] + held[len(held) // 2 * 2 :]
            shift *= 2
        return [(edge, (pl.ds(start, SUB), slice(None)), held[0])]

    for_blocks(count // 2, block, U_EDGE)
    turned = edge[...].T
    size = xsend.shape[0]
    xsend[...] = jnp.concatenate([turned[0 : size - 1], turned[LANES - 1 : LANES]], axis=0)


def transport_kernel(count, rows, cols, single, *refs):
    tan_v, wide, walls, behind = refs[:4]
    adv, ends = refs[-2:]
    comps = 3 * rows
    pairs = ends.shape[0]
    away = towards()
    scale = away.astype(F32)
    arrived = behind[...]
    if not single:
        arrived = jnp.where(iota((SUB, pairs), 0) % 2 == 1, arrived, refs[4][...])
    spare = jnp.zeros((LANES - 3 * SUB, pairs), F32)
    parts = [piece.astype(F32) for piece in pieces(arrived)]
    received = jnp.concatenate(parts + [spare], axis=0).T.astype(BF16)
    r = iota((LANES, ends.shape[1]), 0)
    b = iota((LANES, ends.shape[1]), 1) // LANES
    row_of = jnp.where(b < 2 * rows, (2 * b + SUB - 1) % SUB, 2 * (b - 2 * rows))
    pick = jnp.where((r % SUB == row_of) & (r < 3 * SUB), 1.0, 0.0).astype(BF16)
    ends[...] = dot(received, pick)
    first = iota((SUB, LANES), 0) % 2 == 0
    lane = iota((SUB, LANES), 1)
    wall_row = jnp.where(away == 1, walls[0:1, :], walls[1:2, :]).astype(F32)
    wall = jnp.broadcast_to(wall_row, (SUB, LANES))
    order = [jnp.where(away == 1, k, rows - 1 - k) for k in range(rows)]

    def block(start):
        at = pair_reader(tan_v, comps, rows, start)
        col = lambda j: wide[pl.ds(2 * (j * pairs + start), SUB, stride=2), :]
        vx, ay, sx, toward_sign = (col(j) for j in range(4))
        ax = vx * sx
        sy = toward_sign * scale
        vy3 = 3.0 * (ay * sy)
        even = sx > 0.0
        toward = toward_sign > 0.0
        loaded = [[(at(c, order[k], 0), at(c, order[k], 1)) for c in range(3)] for k in range(rows)]
        results = []
        for side in range(2):
            take = (lambda e, o: jnp.where(even, e, o)) if side == 0 else (lambda e, o: jnp.where(even, o, e))
            center, grad_x, grad_y = ([take(*loaded[k][c]) for k in range(rows)] for c in range(3))
            out_y = [c + sy * g for c, g in zip(center, grad_y)]
            edge_lane = lane == (0 if side == 0 else cols - 1)
            vx3 = 3.0 * ax if side == 0 else -3.0 * ax
            for k in range(rows):
                column = (side * 2 * rows + 2 * order[k]) * LANES
                edge = lambda j: ends[pl.ds(start, SUB), pl.ds(pl.multiple_of(column + j * LANES, LANES), LANES)]
                inflow = lambda piece, j: jnp.where(edge_lane, edge(j), pltpu.roll(piece, 1 if side == 0 else cols - 1, 1))
                out_x = center[k] + grad_x[k] if side == 0 else center[k] - grad_x[k]
                in_x = inflow(out_x, 0)
                in_xs = inflow(grad_y[k], 1)
                if k == 0:
                    near_v = wall * swap_rows(out_y[0], first, 1)
                    near_s = wall * swap_rows(grad_x[0], first, 1)
                else:
                    near_v, near_s = out_y[k - 1], grad_x[k - 1]
                if k == rows - 1:
                    far_v, far_s = jnp.zeros_like(near_v), jnp.zeros_like(near_s)
                else:
                    far_v, far_s = out_y[k + 1], grad_x[k + 1]
                in_y = jnp.where(toward, near_v, far_v)
                in_ys = jnp.where(toward, near_s, far_s)
                twice = 2.0 * center[k]
                results.append(
                    (
                        ax * (out_x - in_x) + ay * (out_y[k] - in_y) + twice,
                        vx3 * (out_x + in_x - twice) + ay * (grad_x[k] - in_ys) + 2.0 * grad_x[k],
                        ax * (grad_y[k] - in_xs) + vy3 * (out_y[k] + in_y - twice) + 2.0 * grad_y[k],
                    )
                )
        stores = []
        for k in range(rows):
            for comp in range(3):
                right, left = results[k][comp], results[rows + k][comp]
                for odd in range(2):
                    value = jnp.where(even, left, right) if odd else jnp.where(even, right, left)
                    where = pl.ds((2 * start + odd) * comps + comp * rows + order[k], SUB, stride=2 * comps)
                    stores.append((adv, (where, slice(None)), value))
        return stores

    for_blocks(count // 2, block, U_TRANS)


def face_terms(yrecv, at, speed, low):
    data = yrecv[pl.ds(at, SUB), :]
    turned = swap_rows(data, low, 2)
    value = speed * jnp.where(low, data, turned)
    slope = speed * jnp.where(low, turned, data)
    return value, slope, (3.0 * towards().astype(F32)) * value


def sym(entries):
    grid = [[None] * 3 for _ in range(3)]
    for k, (i, j) in enumerate(DUOS):
        grid[i][j] = entries[k]
        grid[j][i] = entries[k]
    return grid


def point_params(moments):
    density = moments[0]
    inv_density = 1.0 / density
    u = [moments[1 + i] * inv_density for i in range(3)]
    second = [moments[4 + k] for k in range(6)]
    theta = [second[k] * inv_density - u[i] * u[j] for k, (i, j) in enumerate(DUOS)]
    temp = (theta[0] + theta[1] + theta[2]) / 3.0
    tensor = [(1.5 * temp if i == j else 0.0) - 0.5 * theta[k] for k, (i, j) in enumerate(DUOS)]
    t = sym(tensor)
    cof = [
        t[1][1] * t[2][2] - t[1][2] * t[1][2],
        t[0][0] * t[2][2] - t[0][2] * t[0][2],
        t[0][0] * t[1][1] - t[0][1] * t[0][1],
        t[0][2] * t[1][2] - t[0][1] * t[2][2],
        t[0][1] * t[1][2] - t[0][2] * t[1][1],
        t[0][1] * t[0][2] - t[0][0] * t[1][2],
    ]
    det = t[0][0] * cof[0] + t[0][1] * cof[3] + t[0][2] * cof[4]
    inv_det = 1.0 / det
    inverse = [entry * inv_det for entry in cof]
    log_pre = jnp.log(density) - 1.5 * LOG_TWO_PI - 0.5 * jnp.log(det)
    drho = moments[10]
    du = [(moments[11 + i] - u[i] * drho) * inv_density for i in range(3)]
    ratio = drho * inv_density
    dtheta = [
        moments[14 + k] * inv_density - second[k] * inv_density * ratio - (du[i] * u[j] + u[i] * du[j])
        for k, (i, j) in enumerate(DUOS)
    ]
    dtemp = (dtheta[0] + dtheta[1] + dtheta[2]) / 3.0
    dtensor = [(1.5 * dtemp if i == j else 0.0) - 0.5 * dtheta[k] for k, (i, j) in enumerate(DUOS)]
    a, d = sym(inverse), sym(dtensor)
    trace = sum(a[i][j] * d[j][i] for i in range(3) for j in range(3))
    shift = ratio - 0.5 * trace
    w = [a[i][0] * du[0] + a[i][1] * du[1] + a[i][2] * du[2] for i in range(3)]
    ad = [[a[i][0] * d[0][j] + a[i][1] * d[1][j] + a[i][2] * d[2][j] for j in range(3)] for i in range(3)]
    curve = [ad[i][0] * a[0][j] + ad[i][1] * a[1][j] + ad[i][2] * a[2][j] for i, j in DUOS]
    return u, inverse, log_pre, shift, w, curve


def feature_coefs(const, linear, quad):
    square = [UNIT * UNIT * quad[k] for k in range(6)]
    const = const + square[0] + square[1] + square[2]
    return [const] + [UNIT * l for l in linear] + [4.0 * s for s in square[:3]] + square[3:] + square[3:]


def collide_kernel(count, rows, mom, tab, adv, out_hbm, kept, raw, turn, coef, power, out, sems):
    comps = 3 * rows
    spots = 4 * rows
    weight = SPACING**3
    scales = [weight] + [weight * UNIT] * 3 + [weight * UNIT * UNIT] * 4
    row_scale = jnp.zeros((SUB, LANES), F32)
    sub = iota((SUB, LANES), 0)
    for k, s in enumerate(scales):
        row_scale = jnp.where(sub == k, s, row_scale)
    for a in range(2):
        for row in range(rows):
            first = [row_scale * mom[pl.ds((a * comps + c * rows + row) * 8, 8), :] for c in range(3)]
            last = [
                (weight * UNIT * UNIT) * mom[pl.ds(2 * comps * 8 + (a * comps + c * rows + row) * 2, 2), :]
                for c in range(3)
            ]
            for q in range(4):
                mix = lambda v: v[0] + (XI_SIGNS[q] * GAUSS) * v[1] + (ETA_SIGNS[q] * GAUSS) * v[2]
                base = (q * rows + row) * 24 + a * 10
                raw[pl.ds(base, 8), :] = mix(first)
                raw[pl.ds(base + 8, 2), :] = mix(last)
    moments = [raw[pl.ds(k, spots, stride=24), :] for k in range(20)]
    u, inverse, log_pre, shift, w, curve = point_params(moments)
    a, b = sym(inverse), sym(curve)
    au = [a[i][0] * u[0] + a[i][1] * u[1] + a[i][2] * u[2] for i in range(3)]
    bu = [b[i][0] * u[0] + b[i][1] * u[1] + b[i][2] * u[2] for i in range(3)]
    uau = u[0] * au[0] + u[1] * au[1] + u[2] * au[2]
    ubu = u[0] * bu[0] + u[1] * bu[1] + u[2] * bu[2]
    uw = u[0] * w[0] + u[1] * w[1] + u[2] * w[2]
    half = lambda m, k: (0.5 if k < 3 else 1.0) * m[k]
    expo = feature_coefs(
        LOG2E * (log_pre - 0.5 * uau),
        [LOG2E * v for v in au],
        [-LOG2E * half(inverse, k) for k in range(6)],
    )
    poly = feature_coefs(
        0.5 * (shift - uw + 0.5 * ubu),
        [0.5 * (w[i] - bu[i]) for i in range(3)],
        [0.5 * half(curve, k) for k in range(6)],
    )
    coef[...] = jnp.zeros(coef.shape, BF16)
    for p, entries in enumerate((expo, poly)):
        turn[...] = jnp.zeros(turn.shape, F32)
        for k, entry in enumerate(entries):
            turn[pl.ds(k * spots, spots), :] = entry
        for s in range(spots):
            lanes = pl.ds((p * spots + s) * LANES, LANES)
            for j, piece in enumerate(pieces(turn[pl.ds(s, FEATS, stride=spots), :])):
                coef[pl.ds(j * FEATS, FEATS), lanes] = piece
    root3 = 3.0 * GAUSS
    face = jnp.where(towards() == 1, rows - 1, 0)
    copies = []
    for j, start in enumerate(range(0, count, CHUNK_OUT)):
        size = min(CHUNK_OUT, count - start)
        half_power = power.at[j % 2]
        half_power[...] = dot(tab[pl.ds(start, CHUNK_OUT), :], coef[...])

        def block(local):
            first = (start + local) * comps
            stores = []
            for row in range(rows):
                gd = []
                for q in range(4):
                    lane = (q * rows + row) * LANES
                    expo = half_power[pl.ds(local, SUB), lane : lane + LANES]
                    factor = half_power[pl.ds(local, SUB), spots * LANES + lane : spots * LANES + lane + LANES]
                    gd.append(jnp.exp2(expo) * factor)
                back, front = gd[0] + gd[1], gd[2] + gd[3]
                collided = (back + front, root3 * (front - back), root3 * ((gd[1] - gd[0]) + (gd[3] - gd[2])))
                for comp, value in enumerate(collided):
                    where = pl.ds(first + comp * rows + row, SUB, stride=comps)
                    stores.append((out, (where, slice(None)), adv[where, :] - value))
            return stores

        for_blocks(size, block, U_COLL)
        part = pl.ds(start * comps, size * comps)
        copies.append(pltpu.make_async_copy(out.at[part], out_hbm.at[part], sems.at[j]))
        copies[-1].start()
        part = pl.ds(start * 3, size * 3)
        kept[part, :] = out[pl.ds(start * comps + face, size * 3, stride=rows), :]
    for copy in copies:
        copy.wait()


def face_kernel(count, rows, kept, wide, yrecv, before, out, face_v, sems):
    face = jnp.where(towards() == 1, rows - 1, 0)
    padded = wide.shape[0] // 4
    low = iota((SUB, LANES), 0) % 4 < 2
    copies = []
    for j, start in enumerate(range(0, count, CHUNK_OUT)):
        size = min(CHUNK_OUT, count - start)

        def block(local):
            at = start + local
            ay, toward = (wide[pl.ds(j * padded + at, SUB), :] for j in (1, 3))
            speed = jnp.where(toward > 0.0, 0.0, ay)
            stores = []
            for comp, term in enumerate(face_terms(yrecv, at, speed, low)):
                where = pl.ds(at * 3 + comp, SUB, stride=3)
                stores.append((face_v, (where, slice(None)), kept[where, :] - term))
            return stores

        for_blocks(size, block, U_FACE)
        part = pl.ds(start * 3, size * 3)
        copies.append(pltpu.make_async_copy(face_v.at[part], out.at[part, face], sems.at[j]))
        copies[-1].start()
    for copy in copies:
        copy.wait()


def call(kernel, out_shape, scratch, ins, outs, name, aliases={}, work=0):
    return pl.pallas_call(
        kernel,
        out_shape=out_shape,
        in_specs=[pl.BlockSpec(memory_space=m) for m in ins],
        out_specs=jax.tree.map(lambda m: pl.BlockSpec(memory_space=m), outs),
        scratch_shapes=scratch,
        compiler_params=pltpu.CompilerParams(vmem_limit_bytes=VMEM_LIMIT),
        input_output_aliases=aliases,
        cost_estimate=pl.CostEstimate(flops=work, transcendentals=0, bytes_accessed=0) if work else None,
        name=name,
    )


def exchange(value, axis, by):
    devices = lax.axis_size(axis)
    return lax.ppermute(value, axis, [(i, (i + by) % devices) for i in range(devices)])


def sum_over(value, axis):
    devices = lax.axis_size(axis)
    step = 1
    while step < devices:
        value = value + lax.ppermute(value, axis, [(i, i ^ step) for i in range(devices)])
        step *= 2
    return value


def shards(state, tangent, orient, walls):
    count, _, rows, cols = state.shape
    comps = 3 * rows
    total_rows = count * comps
    padded = roundup(count, CHUNK)
    chunks = padded // CHUNK
    st = state.reshape(total_rows, cols)
    tn = tangent.reshape(total_rows, cols)
    signs = orient.T
    hold = [pltpu.with_memory_space_constraint(v, pltpu.HBM) for v in (signs, tn, st)]
    vm, hbm = pltpu.VMEM, pltpu.HBM
    shape = jax.ShapeDtypeStruct
    ysend, mom, tab, tan_v, wide = call(
        functools.partial(pre_kernel, count, rows),
        (
            shape((count, cols), F32),
            shape((2 * comps * 10, cols), F32),
            shape((padded, LANES), BF16),
            shape((padded * comps, cols), F32),
            shape((4 * padded, LANES), F32),
        ),
        [
            pltpu.VMEM((2, count), jnp.int32),
            pltpu.VMEM((2 * comps * FEATS, cols), F32),
            pltpu.VMEM((FEATS, padded), F32),
            pltpu.VMEM((padded * comps, cols), F32),
            pltpu.SemaphoreType.DMA((2 * chunks + 1,)),
        ],
        (hbm, hbm, hbm),
        (vm, vm, vm, vm, vm),
        "pack_and_moments",
    )(*hold)
    yrecv = lax.ppermute(ysend, "gy", [(0, 1), (1, 0)])
    xsend = call(
        functools.partial(edge_kernel, count, rows),
        shape((SUB, padded // 2), F32),
        [pltpu.VMEM((padded // 2, LANES), F32)],
        (vm, vm),
        vm,
        "edges",
    )(tan_v, wide)
    single = lax.axis_size("gx") == 2
    edges = (exchange(xsend, "gx", 1),) + (() if single else (exchange(xsend, "gx", -1),))
    mom = sum_over(mom, "vert")
    adv = call(
        functools.partial(transport_kernel, count, rows, cols, single),
        shape((total_rows, cols), F32),
        [pltpu.VMEM((padded // 2, 4 * rows * LANES), F32)],
        (vm,) * (3 + len(edges)),
        vm,
        "transport",
        work=WORK,
    )(tan_v, wide, walls, *edges)
    col, kept = call(
        functools.partial(collide_kernel, count, rows),
        (shape((total_rows, cols), F32), shape((count * 3, cols), F32)),
        [
            pltpu.VMEM((4 * rows * 24, LANES), F32),
            pltpu.VMEM((FEATS * 4 * rows, LANES), F32),
            pltpu.VMEM((LANES, 8 * rows * LANES), BF16),
            pltpu.VMEM((2, CHUNK_OUT, 8 * rows * LANES), F32),
            pltpu.VMEM((total_rows, cols), F32),
            pltpu.SemaphoreType.DMA((padded // CHUNK_OUT,)),
        ],
        (vm,) * 3,
        (hbm, vm),
        "collide",
    )(mom, tab, adv)
    out = call(
        functools.partial(face_kernel, count, rows),
        shape((count * 3, rows, cols), F32),
        [
            pltpu.VMEM((count * 3, cols), F32),
            pltpu.SemaphoreType.DMA((padded // CHUNK_OUT,)),
        ],
        (vm, vm, vm, hbm),
        hbm,
        "faces",
        {3: 0},
    )(kept, wide, yrecv, col.reshape(count * 3, rows, cols))
    return out.reshape(state.shape)


def solution(mesh):
    placed = (
        P("vert", None, "gy", "gx"),
        P("vert", None, "gy", "gx"),
        P("vert", None),
        P(None, "gx"),
    )
    return jax.shard_map(
        shards, mesh=mesh, in_specs=placed, out_specs=P("vert", None, "gy", "gx"), check_vma=False
    )
```

```python
import functools
import math

import jax
import jax.numpy as jnp
from jax import lax
from jax.experimental import pallas as pl
from jax.experimental.pallas import tpu as pltpu
from jax.sharding import PartitionSpec as P

NVX = 20
GAUSS = 0.5773502691896258
XI_SIGNS = (-1.0, -1.0, 1.0, 1.0)
ETA_SIGNS = (-1.0, 1.0, -1.0, 1.0)
DUOS = ((0, 0), (1, 1), (2, 2), (0, 1), (0, 2), (1, 2))
LOG_TWO_PI = math.log(2.0 * math.pi)
LOG2E = 1.0 / math.log(2.0)
HALF = NVX // 2
SPACING = 5.0 / HALF
UNIT = 0.5 * SPACING
FEATS = 16
SUB = 8
WORK = 4500 * 10**6
LANES = 128
CHUNK = 512
CHUNK_OUT = 128
U_PACK, U_EDGE, U_TRANS, U_COLL, U_FACE = 64, 31, 16, 16, 16
F32 = jnp.float32
BF16 = jnp.bfloat16
VMEM_LIMIT = 16 * 1024 * 1024


def roundup(value, unit):
    return -(-value // unit) * unit


def for_blocks(count, body, unroll):
    whole = count // SUB
    rounds = whole // unroll

    def group(firsts):
        for ref, where, value in [store for first in firsts for store in body(first)]:
            ref[where] = value

    def step(i, carry):
        group([pl.multiple_of((i * unroll + k) * SUB, SUB) for k in range(unroll)])
        return carry

    if rounds == 1:
        group([k * SUB for k in range(unroll)])
    elif rounds:
        lax.fori_loop(0, rounds, step, 0)
    left = [k * SUB for k in range(rounds * unroll, whole)]
    if left:
        group(left)
    if count % SUB:
        group([count - SUB])


def swap_rows(value, first, by):
    return jnp.where(first, pltpu.roll(value, SUB - by, 0), pltpu.roll(value, by, 0))


def iota(shape, dim):
    return lax.broadcasted_iota(jnp.int32, shape, dim)


def towards():
    return jnp.where(lax.axis_index("gy") == 0, 1, -1)


def fill_features(feat, orient_ref, count):
    feat[...] = jnp.zeros(feat.shape, F32)
    slot = (iota((1, count), 1) + lax.axis_index("vert") * count).astype(F32)
    jz = jnp.floor((slot + 0.5) * (1.0 / (4 * HALF * HALF)))
    slot = slot - jz * (4.0 * HALF * HALF)
    mx = jnp.floor((slot + 0.5) * (1.0 / (4 * HALF)))
    slot = slot - mx * (4.0 * HALF)
    my = jnp.floor((slot + 0.5) * 0.25)
    sx = (2 * orient_ref[0:1, :] - 1).astype(F32)
    sy = (2 * orient_ref[1:2, :] - 1).astype(F32)
    ox = sx * (2.0 * mx + 1.0)
    oy = sy * (2.0 * my + 1.0)
    oz = 2.0 * jz - (2.0 * HALF - 1.0)
    cross = (ox * oy, ox * oz, oy * oz)
    high = [jnp.floor(c * 0.0625) * 16.0 for c in cross]
    low = [c - h for c, h in zip(cross, high)]
    rows = [jnp.ones_like(ox), ox, oy, oz, mx * (mx + 1.0), my * (my + 1.0), 0.25 * (oz * oz - 1.0)]
    rows = rows + high + low + [sx, sy, 2.0 * my + 1.0]
    for k, row in enumerate(rows):
        feat[k : k + 1, 0:count] = row


def spread_table(columns):
    rows = iota((LANES, LANES * len(columns)), 0)
    blocks = iota((LANES, LANES * len(columns)), 1) // LANES
    out = jnp.zeros(rows.shape, F32)
    for j, (row, scale) in enumerate(columns):
        out = jnp.where((rows == row) & (blocks == j), scale, out)
    return out.astype(BF16)


def pieces(value):
    high = value.astype(BF16)
    rest = value - high.astype(F32)
    mid = rest.astype(BF16)
    low = (rest - mid.astype(F32)).astype(BF16)
    return high, mid, low


def dot(left, right):
    return jnp.dot(left, right, preferred_element_type=F32)


def pre_kernel(count, rows, orient_hbm, tan_hbm, st_hbm, ysend, mom, tab, tan_v, wide, orient_ref, total_v, feat, st_v, sems):
    comps = 3 * rows
    padded = feat.shape[1]
    starts = list(range(0, padded, CHUNK))
    copies = []
    for a, (src, dst) in enumerate(((tan_hbm, tan_v), (st_hbm, st_v))):
        for j, start in enumerate(starts):
            size = min(CHUNK, count - start) * comps
            part = pl.ds(start * comps, size)
            copies.append(pltpu.make_async_copy(src.at[part], dst.at[part], sems.at[a * len(starts) + j]))
    signs = pltpu.make_async_copy(orient_hbm, orient_ref, sems.at[2 * len(starts)])
    signs.start()
    for i, copy in enumerate(copies):
        copy.start(priority=0 if i < len(starts) else 1)
    tail = (padded - count) * comps
    for buf in (tan_v, st_v):
        if tail:
            buf[pl.ds(count * comps, tail), :] = jnp.zeros((tail, LANES), F32)
    signs.wait()
    fill_features(feat, orient_ref, count)
    table = feat[...]
    spare = jnp.zeros((LANES - 3 * FEATS, padded), F32)
    flipped = jnp.concatenate([table, table, table, spare], axis=0).T.astype(BF16)
    tab[...] = flipped
    away = towards()
    scale = away.astype(F32)
    for j, column in enumerate(((1, UNIT), (15, UNIT), (13, 1.0), (14, scale))):
        wide[pl.ds(j * padded, padded), :] = dot(flipped, spread_table([column]))
    face = jnp.where(away == 1, rows - 1, 0)
    low = iota((SUB, LANES), 0) % 4 < 2
    table = table.astype(BF16)
    sums = [[total_v.at[pl.ds((a * comps + c) * FEATS, FEATS)] for c in range(comps)] for a in range(2)]
    for a, buf in enumerate((tan_v, st_v)):
        for j, start in enumerate(starts):
            copies[a * len(starts) + j].wait()

            def pack(local):
                first = start + local
                at = lambda comp, row: buf[pl.ds(first * comps + comp * rows + row, SUB, stride=comps), :]
                toward = wide[pl.ds(3 * padded + first, SUB), :]
                center, grad_x, grad_y = at(0, face), at(1, face), at(2, face)
                out_y = center + (toward * scale) * grad_y
                own = jnp.where(low, out_y, grad_x)
                other = jnp.where(low, grad_x, out_y)
                packed = jnp.where(toward > 0.0, own, swap_rows(other, low, 2))
                return [(ysend, (pl.ds(first, SUB), slice(None)), packed)]

            if a == 0:
                for_blocks(min(CHUNK, count - start), pack, U_PACK)
            size = min(CHUNK, padded - start)
            part = table[:, start : start + size]
            for c in range(comps):
                data = buf[pl.ds(start * comps + c, size, stride=comps), :]
                high = data.astype(BF16)
                rest = (data - high.astype(F32)).astype(BF16)
                new = dot(part, high) + dot(part, rest)
                sums[a][c][...] = new if j == 0 else sums[a][c][...] + new
        for c in range(comps):
            total = sums[a][c][...]
            squares = 4.0 * total[4:7] + total[0:1]
            cross = total[7:10] + total[10:13]
            slot = (1 - a) * comps + c
            mom[pl.ds(slot * 8, 4), :] = total[0:4]
            mom[pl.ds(slot * 8 + 4, 3), :] = squares
            mom[pl.ds(slot * 8 + 7, 1), :] = cross[0:1]
            mom[pl.ds(2 * comps * 8 + slot * 2, 2), :] = cross[1:3]


def pair_reader(tan_v, comps, rows, start):
    return lambda comp, row, odd: tan_v[
        pl.ds((2 * start + odd) * comps + comp * rows + row, SUB, stride=2 * comps), :
    ]


def edge_kernel(count, rows, tan_v, wide, xsend, edge):
    comps = 3 * rows
    lane = iota((SUB, LANES), 1)
    last = lane == LANES - 1
    inside = jnp.logical_not(last | (lane == 0))
    sign = jnp.where(last, 1.0, -1.0)
    tail = edge.shape[0] - count // 2
    if tail:
        edge[pl.ds(count // 2, tail), :] = jnp.zeros((tail, LANES), F32)

    def block(start):
        at = pair_reader(tan_v, comps, rows, start)
        even = wide[pl.ds(4 * edge.shape[0] + 2 * start, SUB, stride=2), :] * sign > 0.0
        held = []
        for row in range(rows):
            center, grad_x, grad_y = (jnp.where(even, at(c, row, 0), at(c, row, 1)) for c in range(3))
            held.append(jnp.where(inside, 0.0, center + sign * grad_x))
            held.append(jnp.where(inside, 0.0, grad_y))
        shift = 2
        while len(held) > 1:
            pairs = zip(held[0::2], held[1::2])
            held = [p + pltpu.roll(q, shift, 1) for p, q in pairs] + held[len(held) // 2 * 2 :]
            shift *= 2
        return [(edge, (pl.ds(start, SUB), slice(None)), held[0])]

    for_blocks(count // 2, block, U_EDGE)
    turned = edge[...].T
    size = xsend.shape[0]
    xsend[...] = jnp.concatenate([turned[0 : size - 1], turned[LANES - 1 : LANES]], axis=0)


def transport_kernel(count, rows, cols, single, *refs):
    tan_v, wide, walls, behind = refs[:4]
    adv, ends = refs[-2:]
    comps = 3 * rows
    pairs = ends.shape[0]
    away = towards()
    scale = away.astype(F32)
    arrived = behind[...]
    if not single:
        arrived = jnp.where(iota((SUB, pairs), 0) % 2 == 1, arrived, refs[4][...])
    spare = jnp.zeros((LANES - 3 * SUB, pairs), F32)
    parts = [piece.astype(F32) for piece in pieces(arrived)]
    received = jnp.concatenate(parts + [spare], axis=0).T.astype(BF16)
    r = iota((LANES, ends.shape[1]), 0)
    b = iota((LANES, ends.shape[1]), 1) // LANES
    row_of = jnp.where(b < 2 * rows, (2 * b + SUB - 1) % SUB, 2 * (b - 2 * rows))
    pick = jnp.where((r % SUB == row_of) & (r < 3 * SUB), 1.0, 0.0).astype(BF16)
    ends[...] = dot(received, pick)
    first = iota((SUB, LANES), 0) % 2 == 0
    lane = iota((SUB, LANES), 1)
    wall_row = jnp.where(away == 1, walls[0:1, :], walls[1:2, :]).astype(F32)
    wall = jnp.broadcast_to(wall_row, (SUB, LANES))
    order = [jnp.where(away == 1, k, rows - 1 - k) for k in range(rows)]

    def block(start):
        at = pair_reader(tan_v, comps, rows, start)
        col = lambda j: wide[pl.ds(2 * (j * pairs + start), SUB, stride=2), :]
        vx, ay, sx, toward_sign = (col(j) for j in range(4))
        ax = vx * sx
        sy = toward_sign * scale
        vy3 = 3.0 * (ay * sy)
        even = sx > 0.0
        toward = toward_sign > 0.0
        loaded = [[(at(c, order[k], 0), at(c, order[k], 1)) for c in range(3)] for k in range(rows)]
        results = []
        for side in range(2):
            take = (lambda e, o: jnp.where(even, e, o)) if side == 0 else (lambda e, o: jnp.where(even, o, e))
            center, grad_x, grad_y = ([take(*loaded[k][c]) for k in range(rows)] for c in range(3))
            out_y = [c + sy * g for c, g in zip(center, grad_y)]
            edge_lane = lane == (0 if side == 0 else cols - 1)
            vx3 = 3.0 * ax if side == 0 else -3.0 * ax
            for k in range(rows):
                column = (side * 2 * rows + 2 * order[k]) * LANES
                edge = lambda j: ends[pl.ds(start, SUB), pl.ds(pl.multiple_of(column + j * LANES, LANES), LANES)]
                inflow = lambda piece, j: jnp.where(edge_lane, edge(j), pltpu.roll(piece, 1 if side == 0 else cols - 1, 1))
                out_x = center[k] + grad_x[k] if side == 0 else center[k] - grad_x[k]
                in_x = inflow(out_x, 0)
                in_xs = inflow(grad_y[k], 1)
                if k == 0:
                    near_v = wall * swap_rows(out_y[0], first, 1)
                    near_s = wall * swap_rows(grad_x[0], first, 1)
                else:
                    near_v, near_s = out_y[k - 1], grad_x[k - 1]
                if k == rows - 1:
                    far_v, far_s = jnp.zeros_like(near_v), jnp.zeros_like(near_s)
                else:
                    far_v, far_s = out_y[k + 1], grad_x[k + 1]
                in_y = jnp.where(toward, near_v, far_v)
                in_ys = jnp.where(toward, near_s, far_s)
                twice = 2.0 * center[k]
                results.append(
                    (
                        ax * (out_x - in_x) + ay * (out_y[k] - in_y) + twice,
                        vx3 * (out_x + in_x - twice) + ay * (grad_x[k] - in_ys) + 2.0 * grad_x[k],
                        ax * (grad_y[k] - in_xs) + vy3 * (out_y[k] + in_y - twice) + 2.0 * grad_y[k],
                    )
                )
        stores = []
        for k in range(rows):
            for comp in range(3):
                right, left = results[k][comp], results[rows + k][comp]
                for odd in range(2):
                    value = jnp.where(even, left, right) if odd else jnp.where(even, right, left)
                    where = pl.ds((2 * start + odd) * comps + comp * rows + order[k], SUB, stride=2 * comps)
                    stores.append((adv, (where, slice(None)), value))
        return stores

    for_blocks(count // 2, block, U_TRANS)


def face_terms(yrecv, at, speed, low):
    data = yrecv[pl.ds(at, SUB), :]
    turned = swap_rows(data, low, 2)
    value = speed * jnp.where(low, data, turned)
    slope = speed * jnp.where(low, turned, data)
    return value, slope, (3.0 * towards().astype(F32)) * value


def sym(entries):
    grid = [[None] * 3 for _ in range(3)]
    for k, (i, j) in enumerate(DUOS):
        grid[i][j] = entries[k]
        grid[j][i] = entries[k]
    return grid


def point_params(moments):
    density = moments[0]
    inv_density = 1.0 / density
    u = [moments[1 + i] * inv_density for i in range(3)]
    second = [moments[4 + k] for k in range(6)]
    theta = [second[k] * inv_density - u[i] * u[j] for k, (i, j) in enumerate(DUOS)]
    temp = (theta[0] + theta[1] + theta[2]) / 3.0
    tensor = [(1.5 * temp if i == j else 0.0) - 0.5 * theta[k] for k, (i, j) in enumerate(DUOS)]
    t = sym(tensor)
    cof = [
        t[1][1] * t[2][2] - t[1][2] * t[1][2],
        t[0][0] * t[2][2] - t[0][2] * t[0][2],
        t[0][0] * t[1][1] - t[0][1] * t[0][1],
        t[0][2] * t[1][2] - t[0][1] * t[2][2],
        t[0][1] * t[1][2] - t[0][2] * t[1][1],
        t[0][1] * t[0][2] - t[0][0] * t[1][2],
    ]
    det = t[0][0] * cof[0] + t[0][1] * cof[3] + t[0][2] * cof[4]
    inv_det = 1.0 / det
    inverse = [entry * inv_det for entry in cof]
    log_pre = jnp.log(density) - 1.5 * LOG_TWO_PI - 0.5 * jnp.log(det)
    drho = moments[10]
    du = [(moments[11 + i] - u[i] * drho) * inv_density for i in range(3)]
    ratio = drho * inv_density
    dtheta = [
        moments[14 + k] * inv_density - second[k] * inv_density * ratio - (du[i] * u[j] + u[i] * du[j])
        for k, (i, j) in enumerate(DUOS)
    ]
    dtemp = (dtheta[0] + dtheta[1] + dtheta[2]) / 3.0
    dtensor = [(1.5 * dtemp if i == j else 0.0) - 0.5 * dtheta[k] for k, (i, j) in enumerate(DUOS)]
    a, d = sym(inverse), sym(dtensor)
    trace = sum(a[i][j] * d[j][i] for i in range(3) for j in range(3))
    shift = ratio - 0.5 * trace
    w = [a[i][0] * du[0] + a[i][1] * du[1] + a[i][2] * du[2] for i in range(3)]
    ad = [[a[i][0] * d[0][j] + a[i][1] * d[1][j] + a[i][2] * d[2][j] for j in range(3)] for i in range(3)]
    curve = [ad[i][0] * a[0][j] + ad[i][1] * a[1][j] + ad[i][2] * a[2][j] for i, j in DUOS]
    return u, inverse, log_pre, shift, w, curve


def feature_coefs(const, linear, quad):
    square = [UNIT * UNIT * quad[k] for k in range(6)]
    const = const + square[0] + square[1] + square[2]
    return [const] + [UNIT * l for l in linear] + [4.0 * s for s in square[:3]] + square[3:] + square[3:]


def collide_kernel(count, rows, mom, tab, adv, out_hbm, kept, raw, turn, coef, power, out, sems):
    comps = 3 * rows
    spots = 4 * rows
    weight = SPACING**3
    scales = [weight] + [weight * UNIT] * 3 + [weight * UNIT * UNIT] * 4
    row_scale = jnp.zeros((SUB, LANES), F32)
    sub = iota((SUB, LANES), 0)
    for k, s in enumerate(scales):
        row_scale = jnp.where(sub == k, s, row_scale)
    for a in range(2):
        for row in range(rows):
            first = [row_scale * mom[pl.ds((a * comps + c * rows + row) * 8, 8), :] for c in range(3)]
            last = [
                (weight * UNIT * UNIT) * mom[pl.ds(2 * comps * 8 + (a * comps + c * rows + row) * 2, 2), :]
                for c in range(3)
            ]
            for q in range(4):
                mix = lambda v: v[0] + (XI_SIGNS[q] * GAUSS) * v[1] + (ETA_SIGNS[q] * GAUSS) * v[2]
                base = (q * rows + row) * 24 + a * 10
                raw[pl.ds(base, 8), :] = mix(first)
                raw[pl.ds(base + 8, 2), :] = mix(last)
    moments = [raw[pl.ds(k, spots, stride=24), :] for k in range(20)]
    u, inverse, log_pre, shift, w, curve = point_params(moments)
    a, b = sym(inverse), sym(curve)
    au = [a[i][0] * u[0] + a[i][1] * u[1] + a[i][2] * u[2] for i in range(3)]
    bu = [b[i][0] * u[0] + b[i][1] * u[1] + b[i][2] * u[2] for i in range(3)]
    uau = u[0] * au[0] + u[1] * au[1] + u[2] * au[2]
    ubu = u[0] * bu[0] + u[1] * bu[1] + u[2] * bu[2]
    uw = u[0] * w[0] + u[1] * w[1] + u[2] * w[2]
    half = lambda m, k: (0.5 if k < 3 else 1.0) * m[k]
    expo = feature_coefs(
        LOG2E * (log_pre - 0.5 * uau),
        [LOG2E * v for v in au],
        [-LOG2E * half(inverse, k) for k in range(6)],
    )
    poly = feature_coefs(
        0.5 * (shift - uw + 0.5 * ubu),
        [0.5 * (w[i] - bu[i]) for i in range(3)],
        [0.5 * half(curve, k) for k in range(6)],
    )
    coef[...] = jnp.zeros(coef.shape, BF16)
    for p, entries in enumerate((expo, poly)):
        turn[...] = jnp.zeros(turn.shape, F32)
        for k, entry in enumerate(entries):
            turn[pl.ds(k * spots, spots), :] = entry
        for s in range(spots):
            lanes = pl.ds((p * spots + s) * LANES, LANES)
            for j, piece in enumerate(pieces(turn[pl.ds(s, FEATS, stride=spots), :])):
                coef[pl.ds(j * FEATS, FEATS), lanes] = piece
    root3 = 3.0 * GAUSS
    face = jnp.where(towards() == 1, rows - 1, 0)
    copies = []
    for j, start in enumerate(range(0, count, CHUNK_OUT)):
        size = min(CHUNK_OUT, count - start)
        half_power = power.at[j % 2]
        half_power[...] = dot(tab[pl.ds(start, CHUNK_OUT), :], coef[...])

        def block(local):
            first = (start + local) * comps
            stores = []
            for row in range(rows):
                gd = []
                for q in range(4):
                    lane = (q * rows + row) * LANES
                    expo = half_power[pl.ds(local, SUB), lane : lane + LANES]
                    factor = half_power[pl.ds(local, SUB), spots * LANES + lane : spots * LANES + lane + LANES]
                    gd.append(jnp.exp2(expo) * factor)
                back, front = gd[0] + gd[1], gd[2] + gd[3]
                collided = (back + front, root3 * (front - back), root3 * ((gd[1] - gd[0]) + (gd[3] - gd[2])))
                for comp, value in enumerate(collided):
                    where = pl.ds(first + comp * rows + row, SUB, stride=comps)
                    stores.append((out, (where, slice(None)), adv[where, :] - value))
            return stores

        for_blocks(size, block, U_COLL)
        part = pl.ds(start * comps, size * comps)
        copies.append(pltpu.make_async_copy(out.at[part], out_hbm.at[part], sems.at[j]))
        copies[-1].start()
        part = pl.ds(start * 3, size * 3)
        kept[part, :] = out[pl.ds(start * comps + face, size * 3, stride=rows), :]
    for copy in copies:
        copy.wait()


def face_kernel(count, rows, kept, wide, yrecv, before, out, face_v, sems):
    face = jnp.where(towards() == 1, rows - 1, 0)
    padded = wide.shape[0] // 4
    low = iota((SUB, LANES), 0) % 4 < 2
    copies = []
    for j, start in enumerate(range(0, count, CHUNK_OUT)):
        size = min(CHUNK_OUT, count - start)

        def block(local):
            at = start + local
            ay, toward = (wide[pl.ds(j * padded + at, SUB), :] for j in (1, 3))
            speed = jnp.where(toward > 0.0, 0.0, ay)
            stores = []
            for comp, term in enumerate(face_terms(yrecv, at, speed, low)):
                where = pl.ds(at * 3 + comp, SUB, stride=3)
                stores.append((face_v, (where, slice(None)), kept[where, :] - term))
            return stores

        for_blocks(size, block, U_FACE)
        part = pl.ds(start * 3, size * 3)
        copies.append(pltpu.make_async_copy(face_v.at[part], out.at[part, face], sems.at[j]))
        copies[-1].start()
    for copy in copies:
        copy.wait()


def call(kernel, out_shape, scratch, ins, outs, name, aliases={}, work=0):
    return pl.pallas_call(
        kernel,
        out_shape=out_shape,
        in_specs=[pl.BlockSpec(memory_space=m) for m in ins],
        out_specs=jax.tree.map(lambda m: pl.BlockSpec(memory_space=m), outs),
        scratch_shapes=scratch,
        compiler_params=pltpu.CompilerParams(vmem_limit_bytes=VMEM_LIMIT),
        input_output_aliases=aliases,
        cost_estimate=pl.CostEstimate(flops=work, transcendentals=0, bytes_accessed=0) if work else None,
        name=name,
    )


def exchange(value, axis, by):
    devices = lax.axis_size(axis)
    return lax.ppermute(value, axis, [(i, (i + by) % devices) for i in range(devices)])


def sum_over(value, axis):
    devices = lax.axis_size(axis)
    step = 1
    while step < devices:
        value = value + lax.ppermute(value, axis, [(i, i ^ step) for i in range(devices)])
        step *= 2
    return value


def shards(state, tangent, orient, walls):
    count, _, rows, cols = state.shape
    comps = 3 * rows
    total_rows = count * comps
    padded = roundup(count, CHUNK)
    chunks = padded // CHUNK
    st = state.reshape(total_rows, cols)
    tn = tangent.reshape(total_rows, cols)
    signs = orient.T
    hold = [pltpu.with_memory_space_constraint(v, pltpu.HBM) for v in (signs, tn, st)]
    vm, hbm = pltpu.VMEM, pltpu.HBM
    shape = jax.ShapeDtypeStruct
    ysend, mom, tab, tan_v, wide = call(
        functools.partial(pre_kernel, count, rows),
        (
            shape((count, cols), F32),
            shape((2 * comps * 10, cols), F32),
            shape((padded, LANES), BF16),
            shape((padded * comps, cols), F32),
            shape((4 * padded, LANES), F32),
        ),
        [
            pltpu.VMEM((2, count), jnp.int32),
            pltpu.VMEM((2 * comps * FEATS, cols), F32),
            pltpu.VMEM((FEATS, padded), F32),
            pltpu.VMEM((padded * comps, cols), F32),
            pltpu.SemaphoreType.DMA((2 * chunks + 1,)),
        ],
        (hbm, hbm, hbm),
        (vm, vm, vm, vm, vm),
        "pack_and_moments",
    )(*hold)
    yrecv = lax.ppermute(ysend, "gy", [(0, 1), (1, 0)])
    xsend = call(
        functools.partial(edge_kernel, count, rows),
        shape((SUB, padded // 2), F32),
        [pltpu.VMEM((padded // 2, LANES), F32)],
        (vm, vm),
        vm,
        "edges",
    )(tan_v, wide)
    single = lax.axis_size("gx") == 2
    edges = (exchange(xsend, "gx", 1),) + (() if single else (exchange(xsend, "gx", -1),))
    mom = sum_over(mom, "vert")
    adv = call(
        functools.partial(transport_kernel, count, rows, cols, single),
        shape((total_rows, cols), F32),
        [pltpu.VMEM((padded // 2, 4 * rows * LANES), F32)],
        (vm,) * (3 + len(edges)),
        vm,
        "transport",
        work=WORK,
    )(tan_v, wide, walls, *edges)
    col, kept = call(
        functools.partial(collide_kernel, count, rows),
        (shape((total_rows, cols), F32), shape((count * 3, cols), F32)),
        [
            pltpu.VMEM((4 * rows * 24, LANES), F32),
            pltpu.VMEM((FEATS * 4 * rows, LANES), F32),
            pltpu.VMEM((LANES, 8 * rows * LANES), BF16),
            pltpu.VMEM((2, CHUNK_OUT, 8 * rows * LANES), F32),
            pltpu.VMEM((total_rows, cols), F32),
            pltpu.SemaphoreType.DMA((padded // CHUNK_OUT,)),
        ],
        (vm,) * 3,
        (hbm, vm),
        "collide",
    )(mom, tab, adv)
    out = call(
        functools.partial(face_kernel, count, rows),
        shape((count * 3, rows, cols), F32),
        [
            pltpu.VMEM((count * 3, cols), F32),
            pltpu.SemaphoreType.DMA((padded // CHUNK_OUT,)),
        ],
        (vm, vm, vm, hbm),
        hbm,
        "faces",
        {3: 0},
    )(kept, wide, yrecv, col.reshape(count * 3, rows, cols))
    return out.reshape(state.shape)


def solution(mesh):
    placed = (
        P("vert", None, "gy", "gx"),
        P("vert", None, "gy", "gx"),
        P("vert", None),
        P(None, "gx"),
    )
    return jax.shard_map(
        shards, mesh=mesh, in_specs=placed, out_specs=P("vert", None, "gy", "gx"), check_vma=False
    )
```

```python
import functools
import math

import jax
import jax.numpy as jnp
from jax import lax
from jax.experimental import pallas as pl
from jax.experimental.pallas import tpu as pltpu
from jax.sharding import PartitionSpec as P

NVX = 20
GAUSS = 0.5773502691896258
XI_SIGNS = (-1.0, -1.0, 1.0, 1.0)
ETA_SIGNS = (-1.0, 1.0, -1.0, 1.0)
DUOS = ((0, 0), (1, 1), (2, 2), (0, 1), (0, 2), (1, 2))
LOG_TWO_PI = math.log(2.0 * math.pi)
LOG2E = 1.0 / math.log(2.0)
HALF = NVX // 2
SPACING = 5.0 / HALF
UNIT = 0.5 * SPACING
FEATS = 16
SUB = 8
WORK = 4500 * 10**6
LANES = 128
CHUNK = 512
CHUNK_OUT = 128
U_PACK, U_EDGE, U_TRANS, U_COLL, U_FACE = 64, 31, 16, 16, 16
F32 = jnp.float32
BF16 = jnp.bfloat16
VMEM_LIMIT = 16 * 1024 * 1024


def roundup(value, unit):
    return -(-value // unit) * unit


def for_blocks(count, body, unroll):
    whole = count // SUB
    rounds = whole // unroll

    def group(firsts):
        for ref, where, value in [store for first in firsts for store in body(first)]:
            ref[where] = value

    def step(i, carry):
        group([pl.multiple_of((i * unroll + k) * SUB, SUB) for k in range(unroll)])
        return carry

    if rounds == 1:
        group([k * SUB for k in range(unroll)])
    elif rounds:
        lax.fori_loop(0, rounds, step, 0)
    left = [k * SUB for k in range(rounds * unroll, whole)]
    if left:
        group(left)
    if count % SUB:
        group([count - SUB])


def swap_rows(value, first, by):
    return jnp.where(first, pltpu.roll(value, SUB - by, 0), pltpu.roll(value, by, 0))


def iota(shape, dim):
    return lax.broadcasted_iota(jnp.int32, shape, dim)


def towards():
    return jnp.where(lax.axis_index("gy") == 0, 1, -1)


def fill_features(feat, orient_ref, count):
    feat[...] = jnp.zeros(feat.shape, F32)
    slot = (iota((1, count), 1) + lax.axis_index("vert") * count).astype(F32)
    jz = jnp.floor((slot + 0.5) * (1.0 / (4 * HALF * HALF)))
    slot = slot - jz * (4.0 * HALF * HALF)
    mx = jnp.floor((slot + 0.5) * (1.0 / (4 * HALF)))
    slot = slot - mx * (4.0 * HALF)
    my = jnp.floor((slot + 0.5) * 0.25)
    sx = (2 * orient_ref[0:1, :] - 1).astype(F32)
    sy = (2 * orient_ref[1:2, :] - 1).astype(F32)
    ox = sx * (2.0 * mx + 1.0)
    oy = sy * (2.0 * my + 1.0)
    oz = 2.0 * jz - (2.0 * HALF - 1.0)
    cross = (ox * oy, ox * oz, oy * oz)
    high = [jnp.floor(c * 0.0625) * 16.0 for c in cross]
    low = [c - h for c, h in zip(cross, high)]
    rows = [jnp.ones_like(ox), ox, oy, oz, mx * (mx + 1.0), my * (my + 1.0), 0.25 * (oz * oz - 1.0)]
    rows = rows + high + low + [sx, sy, 2.0 * my + 1.0]
    for k, row in enumerate(rows):
        feat[k : k + 1, 0:count] = row


def spread_table(columns):
    rows = iota((LANES, LANES * len(columns)), 0)
    blocks = iota((LANES, LANES * len(columns)), 1) // LANES
    out = jnp.zeros(rows.shape, F32)
    for j, (row, scale) in enumerate(columns):
        out = jnp.where((rows == row) & (blocks == j), scale, out)
    return out.astype(BF16)


def pieces(value):
    high = value.astype(BF16)
    rest = value - high.astype(F32)
    mid = rest.astype(BF16)
    low = (rest - mid.astype(F32)).astype(BF16)
    return high, mid, low


def dot(left, right):
    return jnp.dot(left, right, preferred_element_type=F32)


def pre_kernel(count, rows, orient_hbm, tan_hbm, st_hbm, ysend, mom, tab, tan_v, wide, orient_ref, total_v, feat, st_v, sems):
    comps = 3 * rows
    padded = feat.shape[1]
    starts = list(range(0, padded, CHUNK))
    copies = []
    for a, (src, dst) in enumerate(((tan_hbm, tan_v), (st_hbm, st_v))):
        for j, start in enumerate(starts):
            size = min(CHUNK, count - start) * comps
            part = pl.ds(start * comps, size)
            copies.append(pltpu.make_async_copy(src.at[part], dst.at[part], sems.at[a * len(starts) + j]))
    signs = pltpu.make_async_copy(orient_hbm, orient_ref, sems.at[2 * len(starts)])
    signs.start()
    for i, copy in enumerate(copies):
        copy.start(priority=0 if i < len(starts) else 1)
    tail = (padded - count) * comps
    for buf in (tan_v, st_v):
        if tail:
            buf[pl.ds(count * comps, tail), :] = jnp.zeros((tail, LANES), F32)
    signs.wait()
    fill_features(feat, orient_ref, count)
    table = feat[...]
    spare = jnp.zeros((LANES - 3 * FEATS, padded), F32)
    flipped = jnp.concatenate([table, table, table, spare], axis=0).T.astype(BF16)
    tab[...] = flipped
    away = towards()
    scale = away.astype(F32)
    for j, column in enumerate(((1, UNIT), (15, UNIT), (13, 1.0), (14, scale))):
        wide[pl.ds(j * padded, padded), :] = dot(flipped, spread_table([column]))
    face = jnp.where(away == 1, rows - 1, 0)
    low = iota((SUB, LANES), 0) % 4 < 2
    table = table.astype(BF16)
    sums = [[total_v.at[pl.ds((a * comps + c) * FEATS, FEATS)] for c in range(comps)] for a in range(2)]
    for a, buf in enumerate((tan_v, st_v)):
        for j, start in enumerate(starts):
            copies[a * len(starts) + j].wait()

            def pack(local):
                first = start + local
                at = lambda comp, row: buf[pl.ds(first * comps + comp * rows + row, SUB, stride=comps), :]
                toward = wide[pl.ds(3 * padded + first, SUB), :]
                center, grad_x, grad_y = at(0, face), at(1, face), at(2, face)
                out_y = center + (toward * scale) * grad_y
                own = jnp.where(low, out_y, grad_x)
                other = jnp.where(low, grad_x, out_y)
                packed = jnp.where(toward > 0.0, own, swap_rows(other, low, 2))
                return [(ysend, (pl.ds(first, SUB), slice(None)), packed)]

            if a == 0:
                for_blocks(min(CHUNK, count - start), pack, U_PACK)
            size = min(CHUNK, padded - start)
            part = table[:, start : start + size]
            for c in range(comps):
                data = buf[pl.ds(start * comps + c, size, stride=comps), :]
                high = data.astype(BF16)
                rest = (data - high.astype(F32)).astype(BF16)
                new = dot(part, high) + dot(part, rest)
                sums[a][c][...] = new if j == 0 else sums[a][c][...] + new
        for c in range(comps):
            total = sums[a][c][...]
            squares = 4.0 * total[4:7] + total[0:1]
            cross = total[7:10] + total[10:13]
            slot = (1 - a) * comps + c
            mom[pl.ds(slot * 8, 4), :] = total[0:4]
            mom[pl.ds(slot * 8 + 4, 3), :] = squares
            mom[pl.ds(slot * 8 + 7, 1), :] = cross[0:1]
            mom[pl.ds(2 * comps * 8 + slot * 2, 2), :] = cross[1:3]


def pair_reader(tan_v, comps, rows, start):
    return lambda comp, row, odd: tan_v[
        pl.ds((2 * start + odd) * comps + comp * rows + row, SUB, stride=2 * comps), :
    ]


def edge_kernel(count, rows, tan_v, wide, xsend, edge):
    comps = 3 * rows
    lane = iota((SUB, LANES), 1)
    last = lane == LANES - 1
    inside = jnp.logical_not(last | (lane == 0))
    sign = jnp.where(last, 1.0, -1.0)
    tail = edge.shape[0] - count // 2
    if tail:
        edge[pl.ds(count // 2, tail), :] = jnp.zeros((tail, LANES), F32)

    def block(start):
        at = pair_reader(tan_v, comps, rows, start)
        even = wide[pl.ds(4 * edge.shape[0] + 2 * start, SUB, stride=2), :] * sign > 0.0
        held = []
        for row in range(rows):
            center, grad_x, grad_y = (jnp.where(even, at(c, row, 0), at(c, row, 1)) for c in range(3))
            held.append(jnp.where(inside, 0.0, center + sign * grad_x))
            held.append(jnp.where(inside, 0.0, grad_y))
        shift = 2
        while len(held) > 1:
            pairs = zip(held[0::2], held[1::2])
            held = [p + pltpu.roll(q, shift, 1) for p, q in pairs] + held[len(held) // 2 * 2 :]
            shift *= 2
        return [(edge, (pl.ds(start, SUB), slice(None)), held[0])]

    for_blocks(count // 2, block, U_EDGE)
    turned = edge[...].T
    size = xsend.shape[0]
    xsend[...] = jnp.concatenate([turned[0 : size - 1], turned[LANES - 1 : LANES]], axis=0)


def transport_kernel(count, rows, cols, single, *refs):
    tan_v, wide, walls, behind = refs[:4]
    adv, ends = refs[-2:]
    comps = 3 * rows
    pairs = ends.shape[0]
    away = towards()
    scale = away.astype(F32)
    arrived = behind[...]
    if not single:
        arrived = jnp.where(iota((SUB, pairs), 0) % 2 == 1, arrived, refs[4][...])
    spare = jnp.zeros((LANES - 3 * SUB, pairs), F32)
    parts = [piece.astype(F32) for piece in pieces(arrived)]
    received = jnp.concatenate(parts + [spare], axis=0).T.astype(BF16)
    r = iota((LANES, ends.shape[1]), 0)
    b = iota((LANES, ends.shape[1]), 1) // LANES
    row_of = jnp.where(b < 2 * rows, (2 * b + SUB - 1) % SUB, 2 * (b - 2 * rows))
    pick = jnp.where((r % SUB == row_of) & (r < 3 * SUB), 1.0, 0.0).astype(BF16)
    ends[...] = dot(received, pick)
    first = iota((SUB, LANES), 0) % 2 == 0
    lane = iota((SUB, LANES), 1)
    wall_row = jnp.where(away == 1, walls[0:1, :], walls[1:2, :]).astype(F32)
    wall = jnp.broadcast_to(wall_row, (SUB, LANES))
    order = [jnp.where(away == 1, k, rows - 1 - k) for k in range(rows)]

    def block(start):
        at = pair_reader(tan_v, comps, rows, start)
        col = lambda j: wide[pl.ds(2 * (j * pairs + start), SUB, stride=2), :]
        vx, ay, sx, toward_sign = (col(j) for j in range(4))
        ax = vx * sx
        sy = toward_sign * scale
        vy3 = 3.0 * (ay * sy)
        even = sx > 0.0
        toward = toward_sign > 0.0
        loaded = [[(at(c, order[k], 0), at(c, order[k], 1)) for c in range(3)] for k in range(rows)]
        results = []
        for side in range(2):
            take = (lambda e, o: jnp.where(even, e, o)) if side == 0 else (lambda e, o: jnp.where(even, o, e))
            center, grad_x, grad_y = ([take(*loaded[k][c]) for k in range(rows)] for c in range(3))
            out_y = [c + sy * g for c, g in zip(center, grad_y)]
            edge_lane = lane == (0 if side == 0 else cols - 1)
            vx3 = 3.0 * ax if side == 0 else -3.0 * ax
            for k in range(rows):
                column = (side * 2 * rows + 2 * order[k]) * LANES
                edge = lambda j: ends[pl.ds(start, SUB), pl.ds(pl.multiple_of(column + j * LANES, LANES), LANES)]
                inflow = lambda piece, j: jnp.where(edge_lane, edge(j), pltpu.roll(piece, 1 if side == 0 else cols - 1, 1))
                out_x = center[k] + grad_x[k] if side == 0 else center[k] - grad_x[k]
                in_x = inflow(out_x, 0)
                in_xs = inflow(grad_y[k], 1)
                if k == 0:
                    near_v = wall * swap_rows(out_y[0], first, 1)
                    near_s = wall * swap_rows(grad_x[0], first, 1)
                else:
                    near_v, near_s = out_y[k - 1], grad_x[k - 1]
                if k == rows - 1:
                    far_v, far_s = jnp.zeros_like(near_v), jnp.zeros_like(near_s)
                else:
                    far_v, far_s = out_y[k + 1], grad_x[k + 1]
                in_y = jnp.where(toward, near_v, far_v)
                in_ys = jnp.where(toward, near_s, far_s)
                twice = 2.0 * center[k]
                results.append(
                    (
                        ax * (out_x - in_x) + ay * (out_y[k] - in_y) + twice,
                        vx3 * (out_x + in_x - twice) + ay * (grad_x[k] - in_ys) + 2.0 * grad_x[k],
                        ax * (grad_y[k] - in_xs) + vy3 * (out_y[k] + in_y - twice) + 2.0 * grad_y[k],
                    )
                )
        stores = []
        for k in range(rows):
            for comp in range(3):
                right, left = results[k][comp], results[rows + k][comp]
                for odd in range(2):
                    value = jnp.where(even, left, right) if odd else jnp.where(even, right, left)
                    where = pl.ds((2 * start + odd) * comps + comp * rows + order[k], SUB, stride=2 * comps)
                    stores.append((adv, (where, slice(None)), value))
        return stores

    for_blocks(count // 2, block, U_TRANS)


def face_terms(yrecv, at, speed, low):
    data = yrecv[pl.ds(at, SUB), :]
    turned = swap_rows(data, low, 2)
    value = speed * jnp.where(low, data, turned)
    slope = speed * jnp.where(low, turned, data)
    return value, slope, (3.0 * towards().astype(F32)) * value


def sym(entries):
    grid = [[None] * 3 for _ in range(3)]
    for k, (i, j) in enumerate(DUOS):
        grid[i][j] = entries[k]
        grid[j][i] = entries[k]
    return grid


def point_params(moments):
    density = moments[0]
    inv_density = 1.0 / density
    u = [moments[1 + i] * inv_density for i in range(3)]
    second = [moments[4 + k] for k in range(6)]
    theta = [second[k] * inv_density - u[i] * u[j] for k, (i, j) in enumerate(DUOS)]
    temp = (theta[0] + theta[1] + theta[2]) / 3.0
    tensor = [(1.5 * temp if i == j else 0.0) - 0.5 * theta[k] for k, (i, j) in enumerate(DUOS)]
    t = sym(tensor)
    cof = [
        t[1][1] * t[2][2] - t[1][2] * t[1][2],
        t[0][0] * t[2][2] - t[0][2] * t[0][2],
        t[0][0] * t[1][1] - t[0][1] * t[0][1],
        t[0][2] * t[1][2] - t[0][1] * t[2][2],
        t[0][1] * t[1][2] - t[0][2] * t[1][1],
        t[0][1] * t[0][2] - t[0][0] * t[1][2],
    ]
    det = t[0][0] * cof[0] + t[0][1] * cof[3] + t[0][2] * cof[4]
    inv_det = 1.0 / det
    inverse = [entry * inv_det for entry in cof]
    log_pre = jnp.log(density) - 1.5 * LOG_TWO_PI - 0.5 * jnp.log(det)
    drho = moments[10]
    du = [(moments[11 + i] - u[i] * drho) * inv_density for i in range(3)]
    ratio = drho * inv_density
    dtheta = [
        moments[14 + k] * inv_density - second[k] * inv_density * ratio - (du[i] * u[j] + u[i] * du[j])
        for k, (i, j) in enumerate(DUOS)
    ]
    dtemp = (dtheta[0] + dtheta[1] + dtheta[2]) / 3.0
    dtensor = [(1.5 * dtemp if i == j else 0.0) - 0.5 * dtheta[k] for k, (i, j) in enumerate(DUOS)]
    a, d = sym(inverse), sym(dtensor)
    trace = sum(a[i][j] * d[j][i] for i in range(3) for j in range(3))
    shift = ratio - 0.5 * trace
    w = [a[i][0] * du[0] + a[i][1] * du[1] + a[i][2] * du[2] for i in range(3)]
    ad = [[a[i][0] * d[0][j] + a[i][1] * d[1][j] + a[i][2] * d[2][j] for j in range(3)] for i in range(3)]
    curve = [ad[i][0] * a[0][j] + ad[i][1] * a[1][j] + ad[i][2] * a[2][j] for i, j in DUOS]
    return u, inverse, log_pre, shift, w, curve


def feature_coefs(const, linear, quad):
    square = [UNIT * UNIT * quad[k] for k in range(6)]
    const = const + square[0] + square[1] + square[2]
    return [const] + [UNIT * l for l in linear] + [4.0 * s for s in square[:3]] + square[3:] + square[3:]


def collide_kernel(count, rows, mom, tab, adv, out_hbm, kept, raw, turn, coef, power, out, sems):
    comps = 3 * rows
    spots = 4 * rows
    weight = SPACING**3
    scales = [weight] + [weight * UNIT] * 3 + [weight * UNIT * UNIT] * 4
    row_scale = jnp.zeros((SUB, LANES), F32)
    sub = iota((SUB, LANES), 0)
    for k, s in enumerate(scales):
        row_scale = jnp.where(sub == k, s, row_scale)
    for a in range(2):
        for row in range(rows):
            first = [row_scale * mom[pl.ds((a * comps + c * rows + row) * 8, 8), :] for c in range(3)]
            last = [
                (weight * UNIT * UNIT) * mom[pl.ds(2 * comps * 8 + (a * comps + c * rows + row) * 2, 2), :]
                for c in range(3)
            ]
            for q in range(4):
                mix = lambda v: v[0] + (XI_SIGNS[q] * GAUSS) * v[1] + (ETA_SIGNS[q] * GAUSS) * v[2]
                base = (q * rows + row) * 24 + a * 10
                raw[pl.ds(base, 8), :] = mix(first)
                raw[pl.ds(base + 8, 2), :] = mix(last)
    moments = [raw[pl.ds(k, spots, stride=24), :] for k in range(20)]
    u, inverse, log_pre, shift, w, curve = point_params(moments)
    a, b = sym(inverse), sym(curve)
    au = [a[i][0] * u[0] + a[i][1] * u[1] + a[i][2] * u[2] for i in range(3)]
    bu = [b[i][0] * u[0] + b[i][1] * u[1] + b[i][2] * u[2] for i in range(3)]
    uau = u[0] * au[0] + u[1] * au[1] + u[2] * au[2]
    ubu = u[0] * bu[0] + u[1] * bu[1] + u[2] * bu[2]
    uw = u[0] * w[0] + u[1] * w[1] + u[2] * w[2]
    half = lambda m, k: (0.5 if k < 3 else 1.0) * m[k]
    expo = feature_coefs(
        LOG2E * (log_pre - 0.5 * uau),
        [LOG2E * v for v in au],
        [-LOG2E * half(inverse, k) for k in range(6)],
    )
    poly = feature_coefs(
        0.5 * (shift - uw + 0.5 * ubu),
        [0.5 * (w[i] - bu[i]) for i in range(3)],
        [0.5 * half(curve, k) for k in range(6)],
    )
    coef[...] = jnp.zeros(coef.shape, BF16)
    for p, entries in enumerate((expo, poly)):
        turn[...] = jnp.zeros(turn.shape, F32)
        for k, entry in enumerate(entries):
            turn[pl.ds(k * spots, spots), :] = entry
        for s in range(spots):
            lanes = pl.ds((p * spots + s) * LANES, LANES)
            for j, piece in enumerate(pieces(turn[pl.ds(s, FEATS, stride=spots), :])):
                coef[pl.ds(j * FEATS, FEATS), lanes] = piece
    root3 = 3.0 * GAUSS
    face = jnp.where(towards() == 1, rows - 1, 0)
    copies = []
    for j, start in enumerate(range(0, count, CHUNK_OUT)):
        size = min(CHUNK_OUT, count - start)
        half_power = power.at[j % 2]
        half_power[...] = dot(tab[pl.ds(start, CHUNK_OUT), :], coef[...])

        def block(local):
            first = (start + local) * comps
            stores = []
            for row in range(rows):
                gd = []
                for q in range(4):
                    lane = (q * rows + row) * LANES
                    expo = half_power[pl.ds(local, SUB), lane : lane + LANES]
                    factor = half_power[pl.ds(local, SUB), spots * LANES + lane : spots * LANES + lane + LANES]
                    gd.append(jnp.exp2(expo) * factor)
                back, front = gd[0] + gd[1], gd[2] + gd[3]
                collided = (back + front, root3 * (front - back), root3 * ((gd[1] - gd[0]) + (gd[3] - gd[2])))
                for comp, value in enumerate(collided):
                    where = pl.ds(first + comp * rows + row, SUB, stride=comps)
                    stores.append((out, (where, slice(None)), adv[where, :] - value))
            return stores

        for_blocks(size, block, U_COLL)
        part = pl.ds(start * comps, size * comps)
        copies.append(pltpu.make_async_copy(out.at[part], out_hbm.at[part], sems.at[j]))
        copies[-1].start()
        part = pl.ds(start * 3, size * 3)
        kept[part, :] = out[pl.ds(start * comps + face, size * 3, stride=rows), :]
    for copy in copies:
        copy.wait()


def face_kernel(count, rows, kept, wide, yrecv, before, out, face_v, sems):
    face = jnp.where(towards() == 1, rows - 1, 0)
    padded = wide.shape[0] // 4
    low = iota((SUB, LANES), 0) % 4 < 2
    copies = []
    for j, start in enumerate(range(0, count, CHUNK_OUT)):
        size = min(CHUNK_OUT, count - start)

        def block(local):
            at = start + local
            ay, toward = (wide[pl.ds(j * padded + at, SUB), :] for j in (1, 3))
            speed = jnp.where(toward > 0.0, 0.0, ay)
            stores = []
            for comp, term in enumerate(face_terms(yrecv, at, speed, low)):
                where = pl.ds(at * 3 + comp, SUB, stride=3)
                stores.append((face_v, (where, slice(None)), kept[where, :] - term))
            return stores

        for_blocks(size, block, U_FACE)
        part = pl.ds(start * 3, size * 3)
        copies.append(pltpu.make_async_copy(face_v.at[part], out.at[part, face], sems.at[j]))
        copies[-1].start(priority=j % 2)
    for copy in copies:
        copy.wait()


def call(kernel, out_shape, scratch, ins, outs, name, aliases={}, work=0):
    return pl.pallas_call(
        kernel,
        out_shape=out_shape,
        in_specs=[pl.BlockSpec(memory_space=m) for m in ins],
        out_specs=jax.tree.map(lambda m: pl.BlockSpec(memory_space=m), outs),
        scratch_shapes=scratch,
        compiler_params=pltpu.CompilerParams(vmem_limit_bytes=VMEM_LIMIT),
        input_output_aliases=aliases,
        cost_estimate=pl.CostEstimate(flops=work, transcendentals=0, bytes_accessed=0) if work else None,
        name=name,
    )


def exchange(value, axis, by):
    devices = lax.axis_size(axis)
    return lax.ppermute(value, axis, [(i, (i + by) % devices) for i in range(devices)])


def sum_over(value, axis):
    devices = lax.axis_size(axis)
    step = 1
    while step < devices:
        value = value + lax.ppermute(value, axis, [(i, i ^ step) for i in range(devices)])
        step *= 2
    return value


def shards(state, tangent, orient, walls):
    count, _, rows, cols = state.shape
    comps = 3 * rows
    total_rows = count * comps
    padded = roundup(count, CHUNK)
    chunks = padded // CHUNK
    st = state.reshape(total_rows, cols)
    tn = tangent.reshape(total_rows, cols)
    signs = orient.T
    hold = [pltpu.with_memory_space_constraint(v, pltpu.HBM) for v in (signs, tn, st)]
    vm, hbm = pltpu.VMEM, pltpu.HBM
    shape = jax.ShapeDtypeStruct
    ysend, mom, tab, tan_v, wide = call(
        functools.partial(pre_kernel, count, rows),
        (
            shape((count, cols), F32),
            shape((2 * comps * 10, cols), F32),
            shape((padded, LANES), BF16),
            shape((padded * comps, cols), F32),
            shape((4 * padded, LANES), F32),
        ),
        [
            pltpu.VMEM((2, count), jnp.int32),
            pltpu.VMEM((2 * comps * FEATS, cols), F32),
            pltpu.VMEM((FEATS, padded), F32),
            pltpu.VMEM((padded * comps, cols), F32),
            pltpu.SemaphoreType.DMA((2 * chunks + 1,)),
        ],
        (hbm, hbm, hbm),
        (vm, vm, vm, vm, vm),
        "pack_and_moments",
    )(*hold)
    yrecv = lax.ppermute(ysend, "gy", [(0, 1), (1, 0)])
    xsend = call(
        functools.partial(edge_kernel, count, rows),
        shape((SUB, padded // 2), F32),
        [pltpu.VMEM((padded // 2, LANES), F32)],
        (vm, vm),
        vm,
        "edges",
    )(tan_v, wide)
    single = lax.axis_size("gx") == 2
    edges = (exchange(xsend, "gx", 1),) + (() if single else (exchange(xsend, "gx", -1),))
    mom = sum_over(mom, "vert")
    adv = call(
        functools.partial(transport_kernel, count, rows, cols, single),
        shape((total_rows, cols), F32),
        [pltpu.VMEM((padded // 2, 4 * rows * LANES), F32)],
        (vm,) * (3 + len(edges)),
        vm,
        "transport",
        work=WORK,
    )(tan_v, wide, walls, *edges)
    col, kept = call(
        functools.partial(collide_kernel, count, rows),
        (shape((total_rows, cols), F32), shape((count * 3, cols), F32)),
        [
            pltpu.VMEM((4 * rows * 24, LANES), F32),
            pltpu.VMEM((FEATS * 4 * rows, LANES), F32),
            pltpu.VMEM((LANES, 8 * rows * LANES), BF16),
            pltpu.VMEM((2, CHUNK_OUT, 8 * rows * LANES), F32),
            pltpu.VMEM((total_rows, cols), F32),
            pltpu.SemaphoreType.DMA((padded // CHUNK_OUT,)),
        ],
        (vm,) * 3,
        (hbm, vm),
        "collide",
    )(mom, tab, adv)
    out = call(
        functools.partial(face_kernel, count, rows),
        shape((count * 3, rows, cols), F32),
        [
            pltpu.VMEM((count * 3, cols), F32),
            pltpu.SemaphoreType.DMA((padded // CHUNK_OUT,)),
        ],
        (vm, vm, vm, hbm),
        hbm,
        "faces",
        {3: 0},
    )(kept, wide, yrecv, col.reshape(count * 3, rows, cols))
    return out.reshape(state.shape)


def solution(mesh):
    placed = (
        P("vert", None, "gy", "gx"),
        P("vert", None, "gy", "gx"),
        P("vert", None),
        P(None, "gx"),
    )
    return jax.shard_map(
        shards, mesh=mesh, in_specs=placed, out_specs=P("vert", None, "gy", "gx"), check_vma=False
    )
```
